512 devices in a mesh: row: 16 (over z_hi, x, core), col: 32 (over y, z_lo).
Axes of the slice: x: 4, y: 4, z: 16 (z_hi: 2, z_lo: 8; z = z_hi * 8 + z_lo), core: 2. Of those that a mesh axis runs over, the one named last changes fastest.
Arguments:
- adjoint: bfloat16 [16, 16, 32, 8, 128, 128], P('row', None, 'col'), may hold values from -0.26367188 to 0.26367188
- features: float32 [32768, 32], P('row'), may hold values from -1.5 to 1.5
- tile_of_slot: int32 [256], replicated, may hold values from 0 to 255, each once
Outputs:
- features_grad: float32 [32768, 32], P('row')
The draws below stay inside these ranges and needn't reach their ends.
Inputs may be any that keep to these rules, and one draw needn't show every extreme that they name: `tile_of_slot`: each tile number appears in exactly one slot.
All inputs are finite; a program needn't handle non-finite values.
Results may differ from the reference program's by a relative error of at most 0.0003.
Values sent between devices are 32-bit elements; how exact they have to be, the bound alone decides.
A program may use at most 64 MiB of HBM per device.

```python
import jax
import jax.numpy as jnp
from jax import lax

FW = 32
B = 128
LTC = 8
LTR = 16
NT = 256
N = 32768
N_ROW = 16
N_COL = 32


def shard_levels(own_key, extent, cuts, low, top_value):
    factor_of, own = 1.0, jax.random.fold_in(own_key, 6)
    for dim, blocks in cuts:
        heights = jnp.exp(jax.random.uniform(jax.random.fold_in(own, dim), (blocks,), jnp.float32, low / len(cuts), top_value / len(cuts)))
        factor_of = factor_of * jnp.repeat(heights, extent[dim] // blocks).reshape([-1 if axis == dim else 1 for axis in range(len(extent))])
    return factor_of


def noise(own_key, shape, spread, reach, cuts=(), held_as=jnp.bfloat16):
    entries = jax.random.normal(own_key, shape, jnp.float32) * spread
    if len(cuts) > 0:
        entries = shard_levels(own_key, shape, cuts, -0.22, 0.18) * entries
    return jnp.clip(entries, min=-reach, max=reach).astype(held_as)


def setup_inputs(seed: int = 0) -> dict:
    arg_keys = jax.random.split(jax.random.key(seed), 4)
    return {
        "adjoint": noise(arg_keys[0], (N_ROW, LTR, N_COL, LTC, B, B), (8.0 / (NT * B) ** 0.5), 0.26367188, ((0, 16), (2, 32))),
        "features": noise(arg_keys[1], (N, FW), 0.25, 1.5, ((0, 16),), jnp.float32),
        "tile_of_slot": jax.random.permutation(arg_keys[2], NT).astype(jnp.int32),
    }


def reference(adjoint, features, tile_of_slot):
    hi = lax.Precision.HIGHEST
    fall = features.reshape(NT, B, FW)
    sq = jnp.sum(fall * fall, axis=-1)
    slots = jnp.arange(NT, dtype=jnp.int32)
    lower = jnp.arange(B)[:, None] >= jnp.arange(B)[None, :]

    def step(carry, s):
        block = lax.dynamic_index_in_dim(adjoint, (s % N_ROW).astype(jnp.int32), 0, False)
        block = lax.dynamic_index_in_dim(block, (s // N_ROW).astype(jnp.int32), 0, False)
        tiles = jnp.transpose(block, (1, 0, 2, 3)).reshape(NT, B, B).astype(jnp.float32)
        frow = fall[s]
        dist = sq[s][None, :, None] + sq[:, None, :] - 2.0 * jnp.einsum("if,ujf->uij", frow, fall, precision=hi)
        kern = jnp.exp(-0.25 * dist)
        live = tile_of_slot[s] > tile_of_slot
        diag = (slots == s)[:, None, None] & lower[None]
        mask = jnp.where(live[:, None, None] | diag, 1.0, 0.0).astype(jnp.float32)
        weight = tiles * kern * mask
        rowpart = jnp.sum(weight, axis=(0, 2))[:, None] * frow - jnp.einsum("uij,ujf->if", weight, fall, precision=hi)
        colpart = jnp.sum(weight, axis=1)[..., None] * fall - jnp.einsum("uij,if->ujf", weight, frow, precision=hi)
        carry = carry + colpart
        carry = carry.at[s].add(rowpart)
        return carry, None

    total, _ = lax.scan(step, jnp.zeros((NT, B, FW), jnp.float32), slots)
    return (-0.5 * total).reshape(NT * B, FW)
```

```python
import functools
import math

import jax
import jax.numpy as jnp
from jax import lax
from jax.experimental import pallas as pl
from jax.experimental.pallas import tpu as pltpu
from jax.sharding import PartitionSpec as P

F32, BF16, I32 = jnp.float32, jnp.bfloat16, jnp.int32
MESH = pl.DeviceIdType.MESH
C0 = 0.5 * math.log2(math.e)
C1 = 0.25 * math.log2(math.e)
NP = 4
NS = 16 // NP
BASE = (8 - NP) // 2
FAR = -1e30


def split3(x):
    h = x.astype(BF16).astype(F32)
    m = (x - h).astype(BF16).astype(F32)
    return h, m, (x - h - m).astype(BF16).astype(F32)


def pick(rows, n):
    sub = lax.broadcasted_iota(I32, (8, n), 0)
    out = jnp.zeros((8, n), F32)
    for k, v in enumerate(rows):
        out = jnp.where(sub == k, v, out)
    return out


def row_operand(f, a):
    h, m, l = split3(C0 * f)
    s = split3(-C1 * jnp.sum(f * f, axis=0, keepdims=True))
    one = jnp.ones_like(s[0])
    hot = (lax.broadcasted_iota(I32, (16, 128), 0) == a).astype(F32)
    return jnp.concatenate([h, h, m, h, m, l, pick([*s, one, one, one], 128), hot, jnp.zeros((40, 128), F32)], axis=0)


def col_operand(f, pen):
    h, m, l = split3(f)
    s = split3(-C1 * jnp.sum(f * f, axis=0, keepdims=True))
    one = jnp.ones_like(s[0])
    return jnp.concatenate([h, m, h, l, m, h, pick([one, one, one, *s], 128), pen, jnp.zeros((40, 128), F32)], axis=0)


def sides(f):
    h, m, _ = split3(f)
    one = pick([jnp.ones((1, 128), F32)], 128)
    pad = jnp.zeros((56, 128), F32)
    return jnp.concatenate([h, m, one, pad], axis=0), jnp.concatenate([h, jnp.zeros((32, 128), F32), one, pad], axis=0)


def dot(a, b):
    return lax.dot_general(a, b, (((1,), (0,)), ((), ())), preferred_element_type=F32)


def dev(zh, x, k, y, zl):
    return (zh * 8 + x * 2 + k, y * 8 + zl)


def push(src, dst, ss, rs, to):
    pltpu.make_async_remote_copy(
        src_ref=src, dst_ref=dst, send_sem=ss, recv_sem=rs, device_id=to, device_id_type=MESH
    ).start()


def arrived(ref, sem):
    pltpu.make_async_copy(ref, ref, sem).wait()


def kernel(
    tos, ft, adj_hbm, out,
    adj, rowf, colf, copb, ctt, acc, rowp, yrecv, ysum, zrecv, colp, krecv, csum, xrecv, c2, crecv, fin,
    s_adj, s_loc, s_row, s_col, s_c4, s_c5, s_far, s_yag, s_yr, s_z, s_k, s_x, s_c, s_ag, s_out, q_in, q_yr, q_z, q_k, q_x, q_c, q_ag,
):
    r = lax.axis_index("row")
    c = lax.axis_index("col")
    zh, x, k = r // 8, lax.rem(r // 2, 4), lax.rem(r, 2)
    y, zl = c // 8, lax.rem(c, 8)
    c16 = lax.rem(c, 16)
    wk = y // 2
    oz = 1 - zh
    pi, rho = lax.rem(r, NP), r // NP
    place = zl - BASE
    final = (place >= 0) & (place < NP)
    edge = (zl == 0) | (zl == 7)
    plane = [(lax.rem(x + d // 2, 4), lax.rem(k + d, 2)) for d in range(1, 8)]
    cpi, crho = lax.rem(c16, NP), c16 // NP

    for j in range(8):
        pltpu.make_async_copy(adj_hbm.at[pl.ds(2 * j, 2)], adj.at[pl.ds(2 * j, 2)], s_adj.at[j]).start()
    pltpu.make_async_copy(ft.at[:, r], rowf.at[:, r], s_loc.at[0]).start()

    @pl.when(k == wk)
    def _():
        pltpu.make_async_copy(ft.at[:, c16], colf.at[:, zh * 4 + x], s_loc.at[1]).start()

    bar = pltpu.get_barrier_semaphore()

    def tell(to):
        pl.semaphore_signal(bar, inc=1, device_id=to, device_id_type=MESH)

    for px, pk in plane:
        tell(dev(zh, px, pk, y, zl))
    for d in range(1, 4):
        tell(dev(zh, x, k, lax.rem(y + d, 4), zl))
    near = jnp.where(zl >= 4, 0, 7)
    for j in range(8):
        tell(dev(oz, j // 2, j % 2, y, near))
    for j in range(NP):
        @pl.when(zl != BASE + j)
        def _():
            tell(dev(zh, x, k, y, BASE + j))

    @pl.when(final)
    def _():
        def rows(j, _):
            q, z = j // 8, lax.rem(j, 8)
            sr = q * NP + place

            @pl.when((sr != r) | (z != zl))
            def _():
                tell((sr, y * 8 + z))
            return 0

        lax.fori_loop(0, NS * 8, rows, 0)

        def cols(j, _):
            q, h = j // 2, lax.rem(j, 2)
            sr = q * NP + place
            sy, sz, sk = 2 * k + sr // 8, lax.rem(sr, 8), y // 2
            to = dev(h, x, sk, sy, sz)

            @pl.when((to[0] != r) | (to[1] != c))
            def _():
                tell(to)
            return 0

        lax.fori_loop(0, NS * 2, cols, 0)

    wait_for = 10 + jnp.where(edge, 32, 0) + 16 + jnp.where(final, 7, 0)
    wait_for -= jnp.where(zl == BASE + pi, 1, 0)
    col_place = BASE + cpi
    col_self = (k == wk) & (zl == col_place) & (y // 2 == k)
    for g in range(2):
        wait_for += jnp.where((k == wk) & (zl == col_place) & (y == 2 * k + g), 1, 2)
    del col_self
    pl.semaphore_wait(bar, wait_for)

    @pl.when(edge)
    def _():
        first = jnp.where(zl == 0, 4, 0)

        @pl.when(k == wk)
        def _():
            for j in range(4):
                push(ft.at[:, lax.rem(y, 2) * 8 + first + j], colf.at[:, zh * 4 + x], q_in.at[0], s_c4, dev(oz, x, k, y, first + j))

        def far(j, _):
            t = oz * 8 + lax.rem(j, 8)
            push(ft.at[y, t], rowf.at[y, r], q_in.at[1], s_far, (t, y * 8 + first + j // 8))
            return 0

        lax.fori_loop(0, 32, far, 0)

    @pl.when(k == wk)
    def _():
        for px, pk in plane:
            push(ft.at[:, c16], colf.at[:, zh * 4 + x], q_in.at[2], s_col, dev(zh, px, pk, y, zl))

    for px, pk in plane:
        push(ft.at[:, zh * 8 + px * 2 + pk], rowf.at[:, r], q_in.at[3], s_row, dev(zh, px, pk, y, zl))

    sub = lax.broadcasted_iota(I32, (16, 128), 0)
    tile = jnp.zeros((16, 128), I32)
    for a in range(16):
        tile = jnp.where(sub == a, tos[a * 16 + r], tile)

    for j in range(8):
        arrived(adj.at[pl.ds(2 * j, 2)], s_adj.at[j])

    @pl.when(r == c16)
    def _():
        low = lax.broadcasted_iota(I32, (128, 128), 0) >= lax.broadcasted_iota(I32, (128, 128), 1)
        for b in range(8):
            a = 2 * b + c // 16
            adj[a, b] = jnp.where(low, adj[a, b].astype(F32), 0.0).astype(BF16)

    acc[...] = jnp.zeros_like(acc)
    arrived(rowf.at[:, r], s_loc.at[0])

    @pl.when(k == wk)
    def _():
        arrived(colf.at[:, zh * 4 + x], s_loc.at[1])
        arrived(colf.at[:, oz * 4 + x], s_c4)
        for px, pk in plane:
            push(colf.at[:, oz * 4 + x], colf.at[:, oz * 4 + x], q_in.at[4], s_c5, dev(zh, px, pk, y, zl))

    arrived(rowf.at[y, pl.ds(oz * 8, 8)], s_far)
    for d in range(1, 4):
        push(rowf.at[y, pl.ds(oz * 8, 8)], rowf.at[y, pl.ds(oz * 8, 8)], q_in.at[5], s_yag.at[d - 1], dev(zh, x, k, lax.rem(y + d, 4), zl))

    @pl.when(k == wk)
    def _():
        arrived(colf.at[:, pl.ds(0, 3)], s_col)
        arrived(colf.at[:, pl.ds(0, 3)], s_c5)

    @pl.when(k != wk)
    def _():
        arrived(colf.at[:, pl.ds(0, 4)], s_col)
        arrived(colf.at[:, pl.ds(0, 4)], s_c5)

    for b in range(8):
        f = colf[:, b].reshape(32, 128)
        ok = (tile > tos[b * 32 + c]) | (sub * 16 + r == b * 32 + c)
        copb[:, b * 128 : (b + 1) * 128] = col_operand(f, jnp.where(ok, 0.0, FAR)).astype(BF16)
        s1, s2 = sides(f)
        ctt[b * 128 : (b + 1) * 128, :] = s1.T.astype(BF16)
        ctt[1024 + b * 128 : 1024 + (b + 1) * 128, :] = s2.T.astype(BF16)

    def pair(j, _):
        a0 = 2 * j
        fs = [rowf[:, a0 + t].reshape(32, 128) for t in range(2)]
        lhs = jnp.concatenate([row_operand(fs[t], a0 + t).T.astype(BF16) for t in range(2)], axis=0)
        sd = [sides(f) for f in fs]
        g = jnp.concatenate([sd[t][u][:80] for u in range(2) for t in range(2)], axis=1).astype(BF16)
        e = jnp.exp2(dot(lhs, copb[...]))
        ad = jnp.concatenate([jnp.concatenate([adj[a0 + t, b] for b in range(8)], axis=1) for t in range(2)], axis=0)
        w = ad.astype(F32) * e
        wh = w.astype(BF16)
        wl = (w - wh.astype(F32)).astype(BF16)
        acc[...] += dot(g, jnp.concatenate([wh, wl], axis=0))
        p = dot(jnp.concatenate([wh, wl], axis=1), ctt[...])
        for t in range(2):
            q = p[t * 128 : (t + 1) * 128].T
            rowp[:, a0 + t] = (q[64:65] * fs[t] - q[0:32] - q[32:64]).reshape(4, 8, 128)
        for d in range(1, 4):
            py = lax.rem(y + d, 4)
            push(rowp.at[py, pl.ds(a0, 2)], yrecv.at[d - 1, pl.ds(a0, 2)], q_yr.at[j], s_yr.at[j], dev(zh, x, k, py, zl))
        return 0

    def settle(j, _):
        a0 = 2 * j
        arrived(yrecv.at[:, pl.ds(a0, 2)], s_yr.at[j])
        two = pl.ds(a0, 2)
        ysum[two] = (rowp[y, two] + yrecv[0, two]) + (yrecv[1, two] + yrecv[2, two])
        for t in range(2):
            a = a0 + t
            here = (a == r) & (zl == BASE + pi)

            @pl.when(here)
            def _():
                cp = pltpu.make_async_copy(ysum.at[a], zrecv.at[rho, zl], s_loc.at[2])
                cp.start()
                cp.wait()

            @pl.when(jnp.logical_not(here))
            def _():
                push(ysum.at[a], zrecv.at[rho, zl], q_z, s_z, (a, y * 8 + BASE + pi))
        return 0

    arrived(rowf.at[:, pl.ds(zh * 8, 7)], s_row)
    lax.fori_loop(zh * 4, zh * 4 + 4, pair, 0)
    for d in range(1, 4):
        arrived(rowf.at[lax.rem(y + 4 - d, 4), pl.ds(oz * 8, 8)], s_yag.at[d - 1])
    lax.fori_loop(zh * 4, zh * 4 + 4, settle, 0)
    lax.fori_loop(oz * 4, oz * 4 + 4, pair, 0)

    for b in range(8):
        q = acc[:, b * 128 : (b + 1) * 128]
        f = colf[:, b].reshape(32, 128)
        colp[:, b] = (q[64:65] * f - q[0:32] - q[32:64]).reshape(4, 8, 128)
    push(colp.at[pl.ds(2 * (1 - k), 2)], krecv, q_k, s_k, dev(zh, x, 1 - k, y, zl))
    arrived(krecv, s_k)
    csum[...] = (colp[pl.ds(2 * k, 2)] + krecv[...]).reshape(2, 2, 4, 8, 128)
    for d in range(1, 4):
        px = lax.rem(x + d, 4)
        push(csum.at[:, :, px], xrecv.at[d - 1], q_x, s_x, dev(zh, px, k, y, zl))
    lax.fori_loop(oz * 4, oz * 4 + 4, settle, 0)
    arrived(xrecv, s_x)
    c2[...] = (csum[:, :, x] + xrecv[0]) + (xrecv[1] + xrecv[2])
    for g in range(2):
        for h in range(2):
            to = dev(h, x, wk, 2 * k + g, col_place)
            here = (to[0] == r) & (to[1] == c)

            @pl.when(here)
            def _():
                cp = pltpu.make_async_copy(c2.at[g, h], crecv.at[crho, zh], s_loc.at[3])
                cp.start()
                cp.wait()

            @pl.when(jnp.logical_not(here))
            def _():
                push(c2.at[g, h], crecv.at[crho, zh], q_c, s_c, to)

    @pl.when(final)
    def _():
        mine = jnp.where(pi == place, 1, 0)

        @pl.when(mine == 1)
        def _():
            arrived(ysum.at[pl.ds(0, 1)], s_z) if NS * 8 == 2 else arrived(zrecv.reshape(NS * 8, 8, 128).at[pl.ds(0, NS * 8 - 1)], s_z)

        @pl.when(mine == 0)
        def _():
            arrived(zrecv, s_z)

        own = (k == wk) & (zl == col_place) & ((y == 2 * k) | (y == 2 * k + 1))

        @pl.when(own)
        def _():
            arrived(crecv.reshape(NS * 2, 8, 128).at[pl.ds(0, NS * 2 - 1)], s_c)

        @pl.when(jnp.logical_not(own))
        def _():
            arrived(crecv, s_c)

        for q in range(NS):
            t = crecv[q, 0] + crecv[q, 1]
            for z in range(8):
                t = t + zrecv[q, z]
            fin[q] = -0.5 * t
        pltpu.make_async_copy(fin, out.at[y, place], s_loc.at[4]).start()
        for d in range(1, 8):
            push(fin, out.at[y, place], q_ag.at[0], s_ag.at[place], dev(zh, x, k, y, lax.rem(zl + d, 8)))
        for d in range(1, 4):
            push(fin, out.at[y, place], q_ag.at[1], s_out.at[d - 1], dev(zh, x, k, lax.rem(y + d, 4), zl))
        arrived(out.at[y, place], s_loc.at[4])

    for j in range(NP):
        @pl.when(zl != BASE + j)
        def _():
            arrived(out.at[y, j], s_ag.at[j])
            for d in range(1, 4):
                push(out.at[y, j], out.at[y, j], q_ag.at[1], s_out.at[d - 1], dev(zh, x, k, lax.rem(y + d, 4), zl))
    for d in range(1, 4):
        arrived(out.at[lax.rem(y + 4 - d, 4)], s_out.at[d - 1])

    @pl.when(edge)
    def _():
        @pl.when(k == wk)
        def _():
            arrived(colf.at[:, pl.ds(0, 4)], q_in.at[0])
        arrived(rowf.at[:, pl.ds(0, 8)], q_in.at[1])

    @pl.when(k == wk)
    def _():
        arrived(colf.at[:, pl.ds(0, 7)], q_in.at[2])
        arrived(colf.at[:, pl.ds(0, 7)], q_in.at[4])
    arrived(colf.at[:, pl.ds(0, 7)], q_in.at[3])
    arrived(rowf.at[pl.ds(0, 3), pl.ds(0, 8)], q_in.at[5])
    for j in range(8):
        arrived(yrecv.at[:, pl.ds(0, 2)], q_yr.at[j])

    @pl.when(zl == BASE + pi)
    def _():
        arrived(ysum.at[pl.ds(0, 15)], q_z)

    @pl.when(zl != BASE + pi)
    def _():
        arrived(ysum, q_z)
    arrived(krecv, q_k)
    arrived(xrecv, q_x)
    own = (k == wk) & (zl == col_place) & ((y == 2 * k) | (y == 2 * k + 1))

    @pl.when(own)
    def _():
        arrived(c2.reshape(4, 8, 128).at[pl.ds(0, 3)], q_c)

    @pl.when(jnp.logical_not(own))
    def _():
        arrived(c2, q_c)

    @pl.when(final)
    def _():
        arrived(ysum.at[pl.ds(0, NS)].reshape(1, NS, 8, 128) if NS * 7 > 16 * 4 else yrecv.reshape(48, 8, 128).at[pl.ds(0, NS * 7)], q_ag.at[0])
    arrived(out.at[pl.ds(0, 3)], q_ag.at[1])


def per_device(adjoint, features, tile_of_slot):
    ft = features.T.reshape(4, 8, 16, 128).transpose(0, 2, 1, 3)
    adj = adjoint.reshape(16, 8, 128, 128)
    anyspace = pl.BlockSpec(memory_space=pl.ANY)
    dma, vm = pltpu.SemaphoreType.DMA, pltpu.VMEM
    out = pl.pallas_call(
        kernel,
        out_shape=jax.ShapeDtypeStruct((4, NP, NS, 8, 128), F32),
        in_specs=[pl.BlockSpec(memory_space=pltpu.SMEM), anyspace, anyspace],
        out_specs=anyspace,
        scratch_shapes=[
            vm((16, 8, 128, 128), BF16),
            vm((4, 16, 8, 128), F32),
            vm((4, 8, 8, 128), F32),
            vm((256, 1024), BF16),
            vm((2048, 128), BF16),
            vm((80, 1024), F32),
            vm((4, 16, 8, 128), F32),
            vm((3, 16, 8, 128), F32),
            vm((16, 8, 128), F32),
            vm((NS, 8, 8, 128), F32),
            vm((4, 8, 8, 128), F32),
            vm((2, 8, 8, 128), F32),
            vm((2, 2, 4, 8, 128), F32),
            vm((3, 2, 2, 8, 128), F32),
            vm((2, 2, 8, 128), F32),
            vm((NS, 2, 8, 128), F32),
            vm((NS, 8, 128), F32),
            dma((8,)), dma((5,)), dma, dma, dma, dma, dma, dma((3,)), dma((8,)), dma, dma, dma, dma, dma((NP,)), dma((3,)),
            dma((6,)), dma((8,)), dma, dma, dma, dma, dma((2,)),
        ],
        compiler_params=pltpu.CompilerParams(collective_id=0, has_side_effects=True, vmem_limit_bytes=60 << 20),
        cost_estimate=pl.CostEstimate(flops=5 * 2**30, bytes_accessed=5 << 20, transcendentals=2 << 20),
        name="gradient",
    )(tile_of_slot, ft, adj)
    return out.transpose(0, 3, 2, 1, 4).reshape(32, 2048).T


def solution(mesh):
    return jax.shard_map(
        per_device,
        mesh=mesh,
        in_specs=(P("row", None, "col", None, None, None), P("row", None), P()),
        out_specs=P("row", None),
        check_vma=False,
    )
```

```python
import functools
import math

import jax
import jax.numpy as jnp
from jax import lax
from jax.experimental import pallas as pl
from jax.experimental.pallas import tpu as pltpu
from jax.sharding import PartitionSpec as P

F32, BF16, I32 = jnp.float32, jnp.bfloat16, jnp.int32
MESH = pl.DeviceIdType.MESH
C0 = 0.5 * math.log2(math.e)
C1 = 0.25 * math.log2(math.e)
NP = 4
NS = 16 // NP
BASE = (8 - NP) // 2
FAR = -1e30


def split3(x):
    h = x.astype(BF16).astype(F32)
    m = (x - h).astype(BF16).astype(F32)
    return h, m, (x - h - m).astype(BF16).astype(F32)


def pick(rows, n):
    sub = lax.broadcasted_iota(I32, (8, n), 0)
    out = jnp.zeros((8, n), F32)
    for k, v in enumerate(rows):
        out = jnp.where(sub == k, v, out)
    return out


def row_operand(f, a):
    h, m, l = split3(C0 * f)
    s = split3(-C1 * jnp.sum(f * f, axis=0, keepdims=True))
    one = jnp.ones_like(s[0])
    hot = (lax.broadcasted_iota(I32, (16, 128), 0) == a).astype(F32)
    return jnp.concatenate([h, h, m, h, m, l, pick([*s, one, one, one], 128), hot, jnp.zeros((40, 128), F32)], axis=0)


def col_operand(f, pen):
    h, m, l = split3(f)
    s = split3(-C1 * jnp.sum(f * f, axis=0, keepdims=True))
    one = jnp.ones_like(s[0])
    return jnp.concatenate([h, m, h, l, m, h, pick([one, one, one, *s], 128), pen, jnp.zeros((40, 128), F32)], axis=0)


def sides(f):
    h, m, _ = split3(f)
    one = pick([jnp.ones((1, 128), F32)], 128)
    pad = jnp.zeros((56, 128), F32)
    return jnp.concatenate([h, m, one, pad], axis=0), jnp.concatenate([h, jnp.zeros((32, 128), F32), one, pad], axis=0)


def dot(a, b):
    return lax.dot_general(a, b, (((1,), (0,)), ((), ())), preferred_element_type=F32)


def dev(zh, x, k, y, zl):
    return (zh * 8 + x * 2 + k, y * 8 + zl)


def push(src, dst, ss, rs, to):
    pltpu.make_async_remote_copy(
        src_ref=src, dst_ref=dst, send_sem=ss, recv_sem=rs, device_id=to, device_id_type=MESH
    ).start()


def arrived(ref, sem):
    pltpu.make_async_copy(ref, ref, sem).wait()


def kernel(
    tos, ft, adj_hbm, out,
    adj, rowf, colf, cop, ctt, lhs, gb, acc, prow, rowp, yrecv, ysum, zrecv, colp, krecv, csum, xrecv, c2, crecv, fin,
    s_adj, s_loc, s_row, s_col, s_c4, s_c5, s_far, s_yag, s_yr, s_z, s_k, s_x, s_c, s_ag, s_out,
    q_in, q_yr, q_z, q_k, q_x, q_c, q_ag, ready,
):
    r = lax.axis_index("row")
    c = lax.axis_index("col")
    zh, x, k = r // 8, lax.rem(r // 2, 4), lax.rem(r, 2)
    y, zl = c // 8, lax.rem(c, 8)
    c16 = lax.rem(c, 16)
    wk = y // 2
    oz = 1 - zh
    pi, rho = lax.rem(r, NP), r // NP
    cpi, crho = lax.rem(c16, NP), c16 // NP
    place = zl - BASE
    final = (place >= 0) & (place < NP)
    edge = (zl == 0) | (zl == 7)
    plane = [dev(zh, lax.rem(x + d // 2, 4), lax.rem(k + d, 2), y, zl) for d in range(1, 8)]
    plane_tile = [zh * 8 + lax.rem(x + d // 2, 4) * 2 + lax.rem(k + d, 2) for d in range(1, 8)]
    ys = [dev(zh, x, k, lax.rem(y + d, 4), zl) for d in range(1, 4)]
    line = []
    for d in (4, 3, 2, 1):
        for z in (lax.rem(zh * 8 + zl + d, 16), lax.rem(zh * 8 + zl + 16 - d, 16)):
            line.append(dev(z // 8, x, k, y, lax.rem(z, 8)))

    bar = pltpu.get_barrier_semaphore()

    def tell(sem, to):
        pl.semaphore_signal(sem, inc=1, device_id=to, device_id_type=MESH)

    near = jnp.where(zl >= 4, 0, 7)
    for j in range(8):
        tell(bar, dev(oz, j // 2, j % 2, y, near))
    for to in line + ys + plane:
        tell(bar, to)
    for j in range(8):
        pltpu.make_async_copy(adj_hbm.at[pl.ds(2 * j, 2)], adj.at[pl.ds(2 * j, 2)], s_adj.at[j]).start()
    pltpu.make_async_copy(ft.at[:, r], rowf.at[:, r], s_loc.at[0]).start()

    @pl.when(k == wk)
    def _():
        pltpu.make_async_copy(ft.at[:, c16], colf.at[:, zh * 4 + x], s_loc.at[1]).start()

    pl.semaphore_wait(bar, 18 + jnp.where(edge, 32, 0))

    @pl.when(edge)
    def _():
        low = jnp.where(zl == 0, 4, 3)
        up = jnp.where(zl == 0, 1, -1)

        @pl.when(k == wk)
        def _():
            for j in range(4):
                z = low + up * j
                push(ft.at[:, lax.rem(y, 2) * 8 + z], colf.at[:, zh * 4 + x], q_in.at[0], s_c4, dev(oz, x, k, y, z))

        def far(j, _):
            t = oz * 8 + lax.rem(j, 8)
            push(ft.at[y, t], rowf.at[y, r], q_in.at[1], s_far, (t, y * 8 + low + up * (j // 8)))
            return 0

        lax.fori_loop(0, 32, far, 0)

    @pl.when(k == wk)
    def _():
        for to in plane:
            push(ft.at[:, c16], colf.at[:, zh * 4 + x], q_in.at[2], s_col, to)

    for to, t in zip(plane, plane_tile, strict=True):
        push(ft.at[:, t], rowf.at[:, r], q_in.at[3], s_row, to)

    for to in line:
        tell(ready.at[0], to)

    sub = lax.broadcasted_iota(I32, (16, 128), 0)
    tile = jnp.zeros((16, 128), I32)
    for a in range(16):
        tile = jnp.where(sub == a, tos[a * 16 + r], tile)

    for j in range(8):
        arrived(adj.at[pl.ds(2 * j, 2)], s_adj.at[j])

    @pl.when(r == c16)
    def _():
        tri = lax.broadcasted_iota(I32, (128, 128), 0) >= lax.broadcasted_iota(I32, (128, 128), 1)
        for b in range(8):
            a = 2 * b + c // 16
            adj[a, b] = jnp.where(tri, adj[a, b].astype(F32), 0.0).astype(BF16)

    acc[...] = jnp.zeros_like(acc)

    def col_side(h):
        for u in range(4):
            b = (zh if h == 0 else oz) * 4 + u
            w = slice(u * 128, (u + 1) * 128)
            f = colf[:, b].reshape(32, 128)
            ok = (tile > tos[b * 32 + c]) | (sub * 16 + r == b * 32 + c)
            cop[h, :, w] = col_operand(f, jnp.where(ok, 0.0, FAR)).astype(BF16)
            s1, s2 = sides(f)
            ctt[h, u * 128 : (u + 1) * 128, :] = s1.T.astype(BF16)
            ctt[h, 512 + u * 128 : 512 + (u + 1) * 128, :] = s2.T.astype(BF16)

    def row_side(i, half):
        for t in range(2):
            a = half * 8 + 2 * i + t
            f = rowf[:, a].reshape(32, 128)
            lhs[i, t * 128 : (t + 1) * 128, :] = row_operand(f, a).T.astype(BF16)
            s1, s2 = sides(f)
            gb[i, :, t * 128 : (t + 1) * 128] = s1[:80].astype(BF16)
            gb[i, :, 256 + t * 128 : 256 + (t + 1) * 128] = s2[:80].astype(BF16)

    def quarter(i, half, h):
        a0 = half * 8 + 2 * i
        b0 = (zh if h == 0 else oz) * 4
        e = jnp.exp2(dot(lhs[i], cop[h]))
        ad = jnp.concatenate([jnp.concatenate([adj[a0 + t, b0 + u] for u in range(4)], axis=1) for t in range(2)], axis=0)
        w = ad.astype(F32) * e
        wh = w.astype(BF16)
        wl = (w - wh.astype(F32)).astype(BF16)
        acc[h] += dot(gb[i], jnp.concatenate([wh, wl], axis=0))
        return dot(jnp.concatenate([wh, wl], axis=1), ctt[h])

    def finish_rows(i, half, p):
        a0 = half * 8 + 2 * i
        for t in range(2):
            q = p[t * 128 : (t + 1) * 128].T
            f = rowf[:, a0 + t].reshape(32, 128)
            rowp[:, a0 + t] = (q[64:65] * f - q[0:32] - q[32:64]).reshape(4, 8, 128)
        two = pl.ds(a0, 2)
        for d in range(1, 4):
            push(rowp.at[lax.rem(y + d, 4), two], yrecv.at[d - 1, two], q_yr.at[a0 // 2], s_yr.at[a0 // 2], ys[d - 1])

    def settle(i, half):
        a0 = half * 8 + 2 * i
        two = pl.ds(a0, 2)
        arrived(yrecv.at[:, two], s_yr.at[a0 // 2])
        ysum[two] = (rowp[y, two] + yrecv[0, two]) + (yrecv[1, two] + yrecv[2, two])
        for t in range(2):
            a = a0 + t
            here = (a == r) & (zl == BASE + pi)

            @pl.when(here)
            def _():
                cp = pltpu.make_async_copy(ysum.at[a], zrecv.at[rho, zl], s_loc.at[2])
                cp.start()
                cp.wait()

            @pl.when(jnp.logical_not(here))
            def _():
                push(ysum.at[a], zrecv.at[rho, zl], q_z, s_z, (a, y * 8 + BASE + pi))

    arrived(rowf.at[:, r], s_loc.at[0])
    arrived(rowf.at[:, pl.ds(zh * 8, 7)], s_row)

    @pl.when(k == wk)
    def _():
        arrived(colf.at[:, zh * 4 + x], s_loc.at[1])
        arrived(colf.at[:, pl.ds(0, 3)], s_col)

    @pl.when(k != wk)
    def _():
        arrived(colf.at[:, pl.ds(0, 4)], s_col)

    col_side(0)

    @pl.when(k == wk)
    def _():
        arrived(colf.at[:, oz * 4 + x], s_c4)
        for to in plane:
            push(colf.at[:, oz * 4 + x], colf.at[:, oz * 4 + x], q_in.at[4], s_c5, to)

    def own_own(i, _):
        row_side(i, zh)
        prow[i] = quarter(i, zh, 0)

        @pl.when(i == 1)
        def _():
            arrived(rowf.at[y, pl.ds(oz * 8, 8)], s_far)
            mine = rowf.at[y, pl.ds(oz * 8, 8)]
            for d in range(1, 4):
                push(mine, mine, q_in.at[5], s_yag.at[d - 1], ys[d - 1])
        return 0

    lax.fori_loop(0, 4, own_own, 0)

    pl.semaphore_wait(ready.at[0], 8)
    for to in plane + ys:
        tell(ready.at[1], to)

    @pl.when(k == wk)
    def _():
        arrived(colf.at[:, pl.ds(0, 3)], s_c5)

    @pl.when(k != wk)
    def _():
        arrived(colf.at[:, pl.ds(0, 4)], s_c5)

    col_side(1)

    def own_other(i, _):
        finish_rows(i, zh, prow[i] + quarter(i, zh, 1))
        return 0

    lax.fori_loop(0, 4, own_other, 0)

    for d in range(1, 4):
        arrived(rowf.at[lax.rem(y + 4 - d, 4), pl.ds(oz * 8, 8)], s_yag.at[d - 1])

    def other_other(i, _):
        row_side(i, oz)
        prow[i] = quarter(i, oz, 1)
        return 0

    lax.fori_loop(0, 4, other_other, 0)

    def col_terms(h):
        half = zh if h == 0 else oz
        for u in range(4):
            q = acc[h, :, u * 128 : (u + 1) * 128]
            f = colf[:, half * 4 + u].reshape(32, 128)
            colp[h, :, u] = (q[64:65] * f - q[0:32] - q[32:64]).reshape(4, 8, 128)

        @pl.when(k != wk)
        def _():
            push(colp.at[h], krecv.at[h], q_k.at[h], s_k.at[h], dev(zh, x, wk, y, zl))

    def col_x(h):
        @pl.when(k == wk)
        def _():
            arrived(krecv.at[h], s_k.at[h])
            csum[h] = colp[h] + krecv[h]
            for d in range(1, 4):
                px = lax.rem(x + d, 4)
                push(csum.at[h, :, px], xrecv.at[h, d - 1], q_x.at[h], s_x.at[h], dev(zh, px, k, y, zl))

    def col_out(h):
        half = zh if h == 0 else oz

        @pl.when(k == wk)
        def _():
            arrived(xrecv.at[h], s_x.at[h])
            c2[h] = (csum[h, :, x] + xrecv[h, 0]) + (xrecv[h, 1] + xrecv[h, 2])
            for g in range(4):
                here = (y == g) & (zl == BASE + cpi) if h == 0 else None
                to = dev(half, x, k, g, BASE + cpi)
                if h == 0:
                    @pl.when(here)
                    def _():
                        cp = pltpu.make_async_copy(c2.at[h, g], crecv.at[crho, zh], s_loc.at[3])
                        cp.start()
                        cp.wait()

                    @pl.when(jnp.logical_not(here))
                    def _():
                        push(c2.at[h, g], crecv.at[crho, zh], q_c, s_c, to)
                else:
                    push(c2.at[h, g], crecv.at[crho, zh], q_c, s_c, to)

    col_terms(1)
    pl.semaphore_wait(ready.at[1], 10)

    def other_own(i, _):
        finish_rows(i, oz, prow[i] + quarter(i, oz, 0))

        @pl.when(i == 1)
        def _():
            col_x(1)
        settle(i, zh)
        return 0

    lax.fori_loop(0, 4, other_own, 0)

    col_terms(0)
    col_x(0)

    settle(0, oz)
    settle(1, oz)

    col_out(1)

    settle(2, oz)
    settle(3, oz)

    col_out(0)

    @pl.when(final)
    def _():
        @pl.when(pi == place)
        def _():
            arrived(zrecv.reshape(NS * 8, 8, 128).at[pl.ds(0, NS * 8 - 1)], s_z)

        @pl.when(pi != place)
        def _():
            arrived(zrecv, s_z)

        @pl.when((k == wk) & (cpi == place))
        def _():
            arrived(crecv.reshape(NS * 2, 8, 128).at[pl.ds(0, NS * 2 - 1)], s_c)

        @pl.when((k != wk) | (cpi != place))
        def _():
            arrived(crecv, s_c)

        for q in range(NS):
            t = crecv[q, 0] + crecv[q, 1]
            for z in range(8):
                t = t + zrecv[q, z]
            fin[q] = -0.5 * t
        pltpu.make_async_copy(fin, out.at[y, :, place], s_loc.at[4]).start()
        for d in range(1, 8):
            push(fin, out.at[y, :, place], q_ag.at[0], s_ag.at[place], dev(zh, x, k, y, lax.rem(zl + d, 8)))
        for d in range(1, 4):
            push(fin, out.at[y, :, place], q_ag.at[1], s_out.at[d - 1], ys[d - 1])
        arrived(out.at[y, :, place], s_loc.at[4])

    for j in range(NP):
        @pl.when(zl != BASE + j)
        def _():
            arrived(out.at[y, :, j], s_ag.at[j])
            for d in range(1, 4):
                push(out.at[y, :, j], out.at[y, :, j], q_ag.at[1], s_out.at[d - 1], ys[d - 1])

    for d in range(1, 4):
        arrived(out.at[lax.rem(y + 4 - d, 4)], s_out.at[d - 1])

    @pl.when(edge)
    def _():
        @pl.when(k == wk)
        def _():
            arrived(colf.at[:, pl.ds(0, 4)], q_in.at[0])
        arrived(rowf.at[:, pl.ds(0, 8)], q_in.at[1])

    @pl.when(k == wk)
    def _():
        arrived(colf.at[:, pl.ds(0, 7)], q_in.at[2])
        arrived(colf.at[:, pl.ds(0, 7)], q_in.at[4])
        for h in range(2):
            arrived(xrecv.at[h], q_x.at[h])

    @pl.when(k != wk)
    def _():
        for h in range(2):
            arrived(krecv.at[h], q_k.at[h])
    arrived(colf.at[:, pl.ds(0, 7)], q_in.at[3])
    arrived(rowf.at[pl.ds(0, 3), pl.ds(0, 8)], q_in.at[5])
    for j in range(8):
        arrived(yrecv.at[:, pl.ds(0, 2)], q_yr.at[j])

    @pl.when(zl == BASE + pi)
    def _():
        arrived(ysum.at[pl.ds(0, 15)], q_z)

    @pl.when(zl != BASE + pi)
    def _():
        arrived(ysum, q_z)

    @pl.when((k == wk) & (zl == BASE + cpi))
    def _():
        arrived(c2.reshape(8, 8, 128).at[pl.ds(0, 7)], q_c)

    @pl.when((k == wk) & (zl != BASE + cpi))
    def _():
        arrived(c2, q_c)

    @pl.when(final)
    def _():
        arrived(zrecv.reshape(NS * 8, 8, 128).at[pl.ds(0, NS * 7)], q_ag.at[0])
    arrived(out.at[pl.ds(0, 3)], q_ag.at[1])


def per_device(adjoint, features, tile_of_slot):
    ft = features.T.reshape(4, 8, 16, 128).transpose(0, 2, 1, 3)
    adj = adjoint.reshape(16, 8, 128, 128)
    anyspace = pl.BlockSpec(memory_space=pl.ANY)
    dma, vm = pltpu.SemaphoreType.DMA, pltpu.VMEM
    out = pl.pallas_call(
        kernel,
        out_shape=jax.ShapeDtypeStruct((4, NS, NP, 8, 128), F32),
        in_specs=[pl.BlockSpec(memory_space=pltpu.SMEM), anyspace, anyspace],
        out_specs=anyspace,
        scratch_shapes=[
            vm((16, 8, 128, 128), BF16),
            vm((4, 16, 8, 128), F32),
            vm((4, 8, 8, 128), F32),
            vm((2, 256, 512), BF16),
            vm((2, 1024, 128), BF16),
            vm((4, 256, 256), BF16),
            vm((4, 80, 512), BF16),
            vm((2, 80, 512), F32),
            vm((4, 256, 128), F32),
            vm((4, 16, 8, 128), F32),
            vm((3, 16, 8, 128), F32),
            vm((16, 8, 128), F32),
            vm((NS, 8, 8, 128), F32),
            vm((2, 4, 4, 8, 128), F32),
            vm((2, 4, 4, 8, 128), F32),
            vm((2, 4, 4, 8, 128), F32),
            vm((2, 3, 4, 8, 128), F32),
            vm((2, 4, 8, 128), F32),
            vm((NS, 2, 8, 128), F32),
            vm((NS, 8, 128), F32),
            dma((8,)), dma((5,)), dma, dma, dma, dma, dma, dma((3,)), dma((8,)), dma, dma((2,)), dma((2,)), dma, dma((NP,)), dma((3,)),
            dma((6,)), dma((8,)), dma, dma((2,)), dma((2,)), dma, dma((2,)), pltpu.SemaphoreType.REGULAR((2,)),
        ],
        compiler_params=pltpu.CompilerParams(collective_id=0, has_side_effects=True, vmem_limit_bytes=60 << 20),
        cost_estimate=pl.CostEstimate(flops=5 * 2**30, bytes_accessed=5 << 20, transcendentals=2 << 20),
        name="gradient",
    )(tile_of_slot, ft, adj)
    return out.reshape(4, 16, 8, 128).transpose(0, 2, 1, 3).reshape(32, 2048).T


def solution(mesh):
    return jax.shard_map(
        per_device,
        mesh=mesh,
        in_specs=(P("row", None, "col", None, None, None), P("row", None), P()),
        out_specs=P("row", None),
        check_vma=False,
    )
```

```python
import functools
import math

import jax
import jax.numpy as jnp
from jax import lax
from jax.experimental import pallas as pl
from jax.experimental.pallas import tpu as pltpu
from jax.sharding import PartitionSpec as P

F32, BF16, I32 = jnp.float32, jnp.bfloat16, jnp.int32
MESH = pl.DeviceIdType.MESH
C0 = 0.5 * math.log2(math.e)
C1 = 0.25 * math.log2(math.e)
NP = 4
NS = 16 // NP
BASE = (8 - NP) // 2
FAR = -1e30


def split3(x):
    h = x.astype(BF16).astype(F32)
    m = (x - h).astype(BF16).astype(F32)
    return h, m, (x - h - m).astype(BF16).astype(F32)


def pick(rows, n):
    sub = lax.broadcasted_iota(I32, (8, n), 0)
    out = jnp.zeros((8, n), F32)
    for k, v in enumerate(rows):
        out = jnp.where(sub == k, v, out)
    return out


def row_operand(f, a):
    h, m, l = split3(C0 * f)
    s = split3(-C1 * jnp.sum(f * f, axis=0, keepdims=True))
    one = jnp.ones_like(s[0])
    hot = (lax.broadcasted_iota(I32, (16, 128), 0) == a).astype(F32)
    return jnp.concatenate([h, h, m, h, m, l, pick([*s, one, one, one], 128), hot, jnp.zeros((40, 128), F32)], axis=0)


def col_operand(f, pen):
    h, m, l = split3(f)
    s = split3(-C1 * jnp.sum(f * f, axis=0, keepdims=True))
    one = jnp.ones_like(s[0])
    return jnp.concatenate([h, m, h, l, m, h, pick([one, one, one, *s], 128), pen, jnp.zeros((40, 128), F32)], axis=0)


def sides(f):
    h, m, _ = split3(f)
    one = pick([jnp.ones((1, 128), F32)], 128)
    pad = jnp.zeros((56, 128), F32)
    return jnp.concatenate([h, m, one, pad], axis=0), jnp.concatenate([h, jnp.zeros((32, 128), F32), one, pad], axis=0)


def dot(a, b):
    return lax.dot_general(a, b, (((1,), (0,)), ((), ())), preferred_element_type=F32)


def dev(zh, x, k, y, zl):
    return (zh * 8 + x * 2 + k, y * 8 + zl)


def push(src, dst, ss, rs, to):
    pltpu.make_async_remote_copy(
        src_ref=src, dst_ref=dst, send_sem=ss, recv_sem=rs, device_id=to, device_id_type=MESH
    ).start()


def arrived(ref, sem):
    pltpu.make_async_copy(ref, ref, sem).wait()


def kernel(
    tos_hbm, ft, adj_hbm, out,
    tos, adj, ftv, rowf, colf, far, zbuf, cop, ctt, lhs, gb, acc, prow, rowp, yrecv, ysum, zrecv, colp, krecv, csum, xrecv, c2, crecv, fin,
    s_adj, s_loc, s_row, s_col, s_c4, s_c5, s_far, s_oth, s_yr, s_z, s_k, s_x, s_c, s_ag, s_out,
    q_in, q_yr, q_z, q_k, q_x, q_c, q_ag, ready,
):
    r = lax.axis_index("row")
    c = lax.axis_index("col")
    zh, x, k = r // 8, lax.rem(r // 2, 4), lax.rem(r, 2)
    y, zl = c // 8, lax.rem(c, 8)
    c16 = lax.rem(c, 16)
    wk = y // 2
    oz = 1 - zh
    pi, rho = lax.rem(r, NP), r // NP
    cpi, crho = lax.rem(c16, NP), c16 // NP
    place = zl - BASE
    final = (place >= 0) & (place < NP)
    edge = (zl == 0) | (zl == 7)
    plane = [dev(zh, lax.rem(x + d // 2, 4), lax.rem(k + d, 2), y, zl) for d in range(1, 8)]
    plane_tile = [zh * 8 + lax.rem(x + d // 2, 4) * 2 + lax.rem(k + d, 2) for d in range(1, 8)]
    ys = [dev(zh, x, k, lax.rem(y + d, 4), zl) for d in range(1, 4)]
    def order(i):
        return lax.rem(x + jnp.where(i == 0, 2, jnp.where(i == 1, 1, jnp.where(i == 2, 3, 0))), 4)

    line = []
    for d in (4, 3, 2, 1):
        for z in (lax.rem(zh * 8 + zl + d, 16), lax.rem(zh * 8 + zl + 16 - d, 16)):
            line.append(dev(z // 8, x, k, y, lax.rem(z, 8)))

    bar = pltpu.get_barrier_semaphore()

    def tell(sem, to):
        pl.semaphore_signal(sem, inc=1, device_id=to, device_id_type=MESH)

    for to in line + ys + plane:
        tell(bar, to)
    for j in range(8):
        pltpu.make_async_copy(adj_hbm.at[pl.ds(2 * j, 2)], adj.at[pl.ds(2 * j, 2)], s_adj.at[j]).start()
    pltpu.make_async_copy(ft, ftv, s_loc.at[0]).start()
    pltpu.make_async_copy(tos_hbm, tos, s_loc.at[1]).start()

    pl.semaphore_wait(bar, 18)
    arrived(ftv, s_loc.at[0])

    @pl.when(edge)
    def _():
        low = jnp.where(zl == 0, 4, 3)
        up = jnp.where(zl == 0, 1, -1)

        for j in range(4):
            z = low + up * j

            @pl.when(k == wk)
            def _():
                push(ftv.at[:, lax.rem(y, 2) * 8 + z], colf.at[:, zh * 4 + x], q_in.at[0], s_c4, dev(oz, x, k, y, z))

        for j in range(4):
            push(ftv.at[y, pl.ds(oz * 8, 8)], far, q_in.at[1], s_far, dev(oz, x, k, y, low + up * j))

    @pl.when(k == wk)
    def _():
        for to in plane:
            push(ftv.at[:, c16], colf.at[:, zh * 4 + x], q_in.at[2], s_col, to)

    for to, t in zip(plane, plane_tile, strict=True):
        push(ftv.at[:, t], rowf.at[:, r], q_in.at[3], s_row, to)

    for to in line + ys:
        tell(ready.at[0], to)
    rowf[:, r] = ftv[:, r]

    @pl.when(k == wk)
    def _():
        colf[:, zh * 4 + x] = ftv[:, c16]

    arrived(tos, s_loc.at[1])
    sub = lax.broadcasted_iota(I32, (16, 128), 0)
    tile = jnp.zeros((16, 128), I32)
    for a in range(16):
        tile = jnp.where(sub == a, tos[a * 16 + r], tile)

    for j in range(8):
        arrived(adj.at[pl.ds(2 * j, 2)], s_adj.at[j])

    @pl.when(r == c16)
    def _():
        tri = lax.broadcasted_iota(I32, (128, 128), 0) >= lax.broadcasted_iota(I32, (128, 128), 1)
        for b in range(8):
            a = 2 * b + c // 16
            adj[a, b] = jnp.where(tri, adj[a, b].astype(F32), 0.0).astype(BF16)

    acc[...] = jnp.zeros_like(acc)

    def col_side(h):
        for u in range(4):
            b = (zh if h == 0 else oz) * 4 + u
            w = slice(u * 128, (u + 1) * 128)
            f = colf[:, b].reshape(32, 128)
            ok = (tile > tos[b * 32 + c]) | (sub * 16 + r == b * 32 + c)
            cop[h, :, w] = col_operand(f, jnp.where(ok, 0.0, FAR)).astype(BF16)
            s1, s2 = sides(f)
            ctt[h, u * 128 : (u + 1) * 128, :] = s1.T.astype(BF16)
            ctt[h, 512 + u * 128 : 512 + (u + 1) * 128, :] = s2.T.astype(BF16)

    def row_side(i, half):
        for t in range(2):
            a = half * 8 + 2 * order(i) + t
            f = rowf[:, a].reshape(32, 128)
            lhs[i, t * 128 : (t + 1) * 128, :] = row_operand(f, a).T.astype(BF16)
            s1, s2 = sides(f)
            gb[i, :, t * 128 : (t + 1) * 128] = s1[:80].astype(BF16)
            gb[i, :, 256 + t * 128 : 256 + (t + 1) * 128] = s2[:80].astype(BF16)

    def quarter(i, half, h):
        a0 = half * 8 + 2 * order(i)
        b0 = (zh if h == 0 else oz) * 4
        e = jnp.exp2(dot(lhs[i], cop[h]))
        ad = jnp.concatenate([jnp.concatenate([adj[a0 + t, b0 + u] for u in range(4)], axis=1) for t in range(2)], axis=0)
        w = ad.astype(F32) * e
        wh = w.astype(BF16)
        wl = (w - wh.astype(F32)).astype(BF16)
        acc[h] += dot(gb[i], jnp.concatenate([wh, wl], axis=0))
        return dot(jnp.concatenate([wh, wl], axis=1), ctt[h])

    def finish_rows(i, half, p):
        a0 = half * 8 + 2 * order(i)
        for t in range(2):
            q = p[t * 128 : (t + 1) * 128].T
            f = rowf[:, a0 + t].reshape(32, 128)
            rowp[:, a0 + t] = (q[64:65] * f - q[0:32] - q[32:64]).reshape(4, 8, 128)
        two = pl.ds(a0, 2)
        for d in range(1, 4):
            push(rowp.at[lax.rem(y + d, 4), two], yrecv.at[d - 1, two], q_yr.at[a0 // 2], s_yr.at[a0 // 2], ys[d - 1])

    def settle(i, half):
        a0 = half * 8 + 2 * order(i)
        two = pl.ds(a0, 2)
        arrived(yrecv.at[:, two], s_yr.at[a0 // 2])
        ysum[two] = (rowp[y, two] + yrecv[0, two]) + (yrecv[1, two] + yrecv[2, two])
        for t in range(2):
            a = a0 + t
            here = (a == r) & (zl == BASE + pi)

            @pl.when(here)
            def _():
                cp = pltpu.make_async_copy(ysum.at[a], zrecv.at[rho, zl], s_loc.at[2])
                cp.start()
                cp.wait()

            @pl.when(jnp.logical_not(here))
            def _():
                push(ysum.at[a], zrecv.at[rho, zl], q_z, s_z, (a, y * 8 + BASE + pi))

    arrived(rowf.at[:, pl.ds(zh * 8, 7)], s_row)

    @pl.when(k == wk)
    def _():
        arrived(colf.at[:, pl.ds(0, 3)], s_col)

    @pl.when(k != wk)
    def _():
        arrived(colf.at[:, pl.ds(0, 4)], s_col)

    col_side(0)

    @pl.when(k == wk)
    def _():
        arrived(colf.at[:, oz * 4 + x], s_c4)
        for to in plane:
            push(colf.at[:, oz * 4 + x], colf.at[:, oz * 4 + x], q_in.at[4], s_c5, to)

    def own_own(i, _):
        row_side(i, zh)
        prow[i] = quarter(i, zh, 0)
        return 0

    lax.fori_loop(0, 4, own_own, 0, unroll=2)

    pl.semaphore_wait(ready.at[0], 11)

    arrived(far, s_far)
    oth = oz * 8 + x * 2 + k
    rowf[y, oth] = far[x * 2 + k]
    spots = [(x * 2 + k, (r, c))] + [(t - zh * 8, to) for to, t in zip(plane, plane_tile, strict=True)]
    for spot, to in spots:
        for d in range(4):
            if spot is not spots[0][0] or d:
                push(far.at[spot], rowf.at[y, oth], q_in.at[5], s_oth, (to[0], lax.rem(y + d, 4) * 8 + zl))

    for to in plane + ys:
        tell(ready.at[1], to)

    @pl.when(k == wk)
    def _():
        arrived(colf.at[:, pl.ds(0, 3)], s_c5)

    @pl.when(k != wk)
    def _():
        arrived(colf.at[:, pl.ds(0, 4)], s_c5)

    col_side(1)

    def own_other(i, _):
        finish_rows(i, zh, prow[i] + quarter(i, zh, 1))
        return 0

    lax.fori_loop(0, 4, own_other, 0, unroll=2)

    arrived(yrecv.reshape(48, 8, 128).at[pl.ds(0, 31)], s_oth)

    def other_other(i, _):
        row_side(i, oz)
        prow[i] = quarter(i, oz, 1)
        return 0

    lax.fori_loop(0, 4, other_other, 0, unroll=2)

    def col_terms(h):
        half = zh if h == 0 else oz
        for u in range(4):
            q = acc[h, :, u * 128 : (u + 1) * 128]
            f = colf[:, half * 4 + u].reshape(32, 128)
            colp[h, :, u] = (q[64:65] * f - q[0:32] - q[32:64]).reshape(4, 8, 128)

        @pl.when(k != wk)
        def _():
            push(colp.at[h], krecv.at[h], q_k.at[h], s_k.at[h], dev(zh, x, wk, y, zl))

    def col_x(h):
        @pl.when(k == wk)
        def _():
            arrived(krecv.at[h], s_k.at[h])
            csum[h] = colp[h] + krecv[h]
            for d in range(1, 4):
                px = lax.rem(x + d, 4)
                push(csum.at[h, :, px], xrecv.at[h, d - 1], q_x.at[h], s_x.at[h], dev(zh, px, k, y, zl))

    def col_out(h):
        half = zh if h == 0 else oz

        @pl.when(k == wk)
        def _():
            arrived(xrecv.at[h], s_x.at[h])
            c2[h] = (csum[h, :, x] + xrecv[h, 0]) + (xrecv[h, 1] + xrecv[h, 2])
            for g in range(4):
                here = (y == g) & (zl == BASE + cpi) if h == 0 else None
                to = dev(half, x, k, g, BASE + cpi)
                if h == 0:
                    @pl.when(here)
                    def _():
                        cp = pltpu.make_async_copy(c2.at[h, g], crecv.at[crho, zh], s_loc.at[3])
                        cp.start()
                        cp.wait()

                    @pl.when(jnp.logical_not(here))
                    def _():
                        push(c2.at[h, g], crecv.at[crho, zh], q_c, s_c, to)
                else:
                    push(c2.at[h, g], crecv.at[crho, zh], q_c, s_c, to)

    col_terms(1)
    pl.semaphore_wait(ready.at[1], 10)

    def other_own(i, _):
        finish_rows(i, oz, prow[i] + quarter(i, oz, 0))

        @pl.when(i == 1)
        def _():
            col_x(1)
        settle(i, zh)
        return 0

    lax.fori_loop(0, 4, other_own, 0, unroll=2)

    col_terms(0)
    col_x(0)

    settle(0, oz)
    settle(1, oz)

    col_out(1)

    settle(2, oz)
    settle(3, oz)

    col_out(0)

    @pl.when(final)
    def _():
        @pl.when(pi == place)
        def _():
            arrived(zrecv.reshape(NS * 8, 8, 128).at[pl.ds(0, NS * 8 - 1)], s_z)

        @pl.when(pi != place)
        def _():
            arrived(zrecv, s_z)

        @pl.when((k == wk) & (cpi == place))
        def _():
            arrived(crecv.reshape(NS * 2, 8, 128).at[pl.ds(0, NS * 2 - 1)], s_c)

        @pl.when((k != wk) | (cpi != place))
        def _():
            arrived(crecv, s_c)

        for q in range(NS):
            t = crecv[q, 0] + crecv[q, 1]
            for z in range(8):
                t = t + zrecv[q, z]
            fin[q] = -0.5 * t
            zbuf[q, place] = -0.5 * t
        for d in (5, 3, 4, 2, 6, 1, 7):
            push(fin, zbuf.at[:, place], q_ag.at[0], s_ag.at[place], dev(zh, x, k, y, lax.rem(zl + d, 8)))
        for d in range(1, 4):
            push(fin, out.at[y, :, place], q_ag.at[1], s_out.at[d - 1], ys[d - 1])

    for j in range(NP):
        @pl.when(zl != BASE + j)
        def _():
            arrived(zbuf.at[:, j], s_ag.at[j])
            for d in range(1, 4):
                push(zbuf.at[:, j], out.at[y, :, j], q_ag.at[1], s_out.at[d - 1], ys[d - 1])

    pltpu.make_async_copy(zbuf, out.at[y], s_loc.at[4]).start()
    for d in range(1, 4):
        arrived(out.at[lax.rem(y + 4 - d, 4)], s_out.at[d - 1])

    arrived(zbuf, s_loc.at[4])

    @pl.when(edge)
    def _():
        @pl.when(k == wk)
        def _():
            arrived(colf.at[:, pl.ds(0, 4)], q_in.at[0])
        arrived(rowf.at[:, pl.ds(0, 8)], q_in.at[1])

    @pl.when(k == wk)
    def _():
        arrived(colf.at[:, pl.ds(0, 7)], q_in.at[2])
        arrived(colf.at[:, pl.ds(0, 7)], q_in.at[4])
        for h in range(2):
            arrived(xrecv.at[h], q_x.at[h])

    @pl.when(k != wk)
    def _():
        for h in range(2):
            arrived(krecv.at[h], q_k.at[h])
    arrived(colf.at[:, pl.ds(0, 7)], q_in.at[3])
    arrived(yrecv.reshape(48, 8, 128).at[pl.ds(0, 31)], q_in.at[5])
    for j in range(8):
        arrived(yrecv.at[:, pl.ds(0, 2)], q_yr.at[j])

    @pl.when(zl == BASE + pi)
    def _():
        arrived(ysum.at[pl.ds(0, 15)], q_z)

    @pl.when(zl != BASE + pi)
    def _():
        arrived(ysum, q_z)

    @pl.when((k == wk) & (zl == BASE + cpi))
    def _():
        arrived(c2.reshape(8, 8, 128).at[pl.ds(0, 7)], q_c)

    @pl.when((k == wk) & (zl != BASE + cpi))
    def _():
        arrived(c2, q_c)

    @pl.when(final)
    def _():
        arrived(zrecv.reshape(NS * 8, 8, 128).at[pl.ds(0, NS * 7)], q_ag.at[0])
    arrived(out.at[pl.ds(0, 3)], q_ag.at[1])


def per_device(adjoint, features, tile_of_slot):
    ft = features.T.reshape(4, 8, 16, 128).transpose(0, 2, 1, 3)
    adj = adjoint.reshape(16, 8, 128, 128)
    anyspace = pl.BlockSpec(memory_space=pl.ANY)
    dma, vm = pltpu.SemaphoreType.DMA, pltpu.VMEM
    out = pl.pallas_call(
        kernel,
        out_shape=jax.ShapeDtypeStruct((4, NS, NP, 8, 128), F32),
        in_specs=[anyspace] * 3,
        out_specs=anyspace,
        scratch_shapes=[
            pltpu.SMEM((256,), I32),
            vm((16, 8, 128, 128), BF16),
            vm((4, 16, 8, 128), F32),
            vm((4, 16, 8, 128), F32),
            vm((4, 8, 8, 128), F32),
            vm((8, 8, 128), F32),
            vm((NS, NP, 8, 128), F32),
            vm((2, 256, 512), BF16),
            vm((2, 1024, 128), BF16),
            vm((4, 256, 256), BF16),
            vm((4, 80, 512), BF16),
            vm((2, 80, 512), F32),
            vm((4, 256, 128), F32),
            vm((4, 16, 8, 128), F32),
            vm((3, 16, 8, 128), F32),
            vm((16, 8, 128), F32),
            vm((NS, 8, 8, 128), F32),
            vm((2, 4, 4, 8, 128), F32),
            vm((2, 4, 4, 8, 128), F32),
            vm((2, 4, 4, 8, 128), F32),
            vm((2, 3, 4, 8, 128), F32),
            vm((2, 4, 8, 128), F32),
            vm((NS, 2, 8, 128), F32),
            vm((NS, 8, 128), F32),
            dma((8,)), dma((5,)), dma, dma, dma, dma, dma, dma, dma((8,)), dma, dma((2,)), dma((2,)), dma, dma((NP,)), dma((3,)),
            dma((6,)), dma((8,)), dma, dma((2,)), dma((2,)), dma, dma((2,)), pltpu.SemaphoreType.REGULAR((2,)),
        ],
        compiler_params=pltpu.CompilerParams(collective_id=0, has_side_effects=True, vmem_limit_bytes=60 << 20),
        cost_estimate=pl.CostEstimate(flops=5 * 2**30, bytes_accessed=5 << 20, transcendentals=2 << 20),
        name="gradient",
    )(tile_of_slot, ft, adj)
    return out.reshape(4, 16, 8, 128).transpose(0, 2, 1, 3).reshape(32, 2048).T


def solution(mesh):
    return jax.shard_map(
        per_device,
        mesh=mesh,
        in_specs=(P("row", None, "col", None, None, None), P("row", None), P()),
        out_specs=P("row", None),
        check_vma=False,
    )
```

```python
import functools
import math

import jax
import jax.numpy as jnp
from jax import lax
from jax.experimental import pallas as pl
from jax.experimental.pallas import tpu as pltpu
from jax.sharding import PartitionSpec as P

F32, BF16, I32 = jnp.float32, jnp.bfloat16, jnp.int32
MESH = pl.DeviceIdType.MESH
C0 = 0.5 * math.log2(math.e)
C1 = 0.25 * math.log2(math.e)
NP = 4
NS = 16 // NP
FAR = -1e30


def split3(x):
    h = x.astype(BF16).astype(F32)
    m = (x - h).astype(BF16).astype(F32)
    return h, m, (x - h - m).astype(BF16).astype(F32)


def pick(rows, n):
    sub = lax.broadcasted_iota(I32, (8, n), 0)
    out = jnp.zeros((8, n), F32)
    for k, v in enumerate(rows):
        out = jnp.where(sub == k, v, out)
    return out


def row_operand(f, a):
    h, m, l = split3(C0 * f)
    s = split3(-C1 * jnp.sum(f * f, axis=0, keepdims=True))
    one = jnp.ones_like(s[0])
    hot = (lax.broadcasted_iota(I32, (16, 128), 0) == a).astype(F32)
    return jnp.concatenate([h, h, m, h, m, l, pick([*s, one, one, one], 128), hot, jnp.zeros((40, 128), F32)], axis=0)


def col_operand(f, pen):
    h, m, l = split3(f)
    s = split3(-C1 * jnp.sum(f * f, axis=0, keepdims=True))
    one = jnp.ones_like(s[0])
    return jnp.concatenate([h, m, h, l, m, h, pick([one, one, one, *s], 128), pen, jnp.zeros((40, 128), F32)], axis=0)


def sides(f):
    h, m, _ = split3(f)
    one = pick([jnp.ones((1, 128), F32)], 128)
    pad = jnp.zeros((56, 128), F32)
    return jnp.concatenate([h, m, one, pad], axis=0), jnp.concatenate([h, jnp.zeros((32, 128), F32), one, pad], axis=0)


def dot(a, b):
    return lax.dot_general(a, b, (((1,), (0,)), ((), ())), preferred_element_type=F32)


def base(zh):
    return 1 + zh


def dev(zh, x, k, y, zl):
    return (zh * 8 + x * 2 + k, y * 8 + zl)


def push(src, dst, ss, rs, to):
    pltpu.make_async_remote_copy(
        src_ref=src, dst_ref=dst, send_sem=ss, recv_sem=rs, device_id=to, device_id_type=MESH
    ).start()


def arrived(ref, sem):
    pltpu.make_async_copy(ref, ref, sem).wait()


def kernel(
    tos_hbm, ft, adj_hbm, out,
    tos, adj, ftv, rowf, colf, far, zbuf, cop, ctt, lhs, gb, acc, prow, rowp, yrecv, ysum, zrecv, colp, krecv, csum, xrecv, c2, crecv, fin,
    s_adj, s_loc, s_row, s_col, s_c4, s_c5, s_far, s_oth, s_yr, s_z, s_k, s_x, s_c, s_ag, s_out,
    q_in, q_yr, q_z, q_k, q_x, q_c, q_ag, ready,
):
    r = lax.axis_index("row")
    c = lax.axis_index("col")
    zh, x, k = r // 8, lax.rem(r // 2, 4), lax.rem(r, 2)
    y, zl = c // 8, lax.rem(c, 8)
    c16 = lax.rem(c, 16)
    wk = y // 2
    oz = 1 - zh
    pi, rho = lax.rem(r, NP), r // NP
    cpi, crho = lax.rem(c16, NP), c16 // NP
    place = zl - base(zh)
    final = (place >= 0) & (place < NP)
    edge = (zl == 0) | (zl == 7)
    plane = [dev(zh, lax.rem(x + d // 2, 4), lax.rem(k + d, 2), y, zl) for d in range(1, 8)]
    plane_tile = [zh * 8 + lax.rem(x + d // 2, 4) * 2 + lax.rem(k + d, 2) for d in range(1, 8)]
    ys = [dev(zh, x, k, lax.rem(y + d, 4), zl) for d in range(1, 4)]
    def order(i):
        return lax.rem(x + jnp.where(i == 0, 2, jnp.where(i == 1, 1, jnp.where(i == 2, 3, 0))), 4)

    line = []
    for d in (4, 3, 2, 1):
        for z in (lax.rem(zh * 8 + zl + d, 16), lax.rem(zh * 8 + zl + 16 - d, 16)):
            line.append(dev(z // 8, x, k, y, lax.rem(z, 8)))

    bar = pltpu.get_barrier_semaphore()

    def tell(sem, to):
        pl.semaphore_signal(sem, inc=1, device_id=to, device_id_type=MESH)

    for to in line + ys + plane:
        tell(bar, to)
    for j in range(8):
        pltpu.make_async_copy(adj_hbm.at[pl.ds(2 * j, 2)], adj.at[pl.ds(2 * j, 2)], s_adj.at[j]).start()
    pltpu.make_async_copy(ft, ftv, s_loc.at[0]).start()
    pltpu.make_async_copy(tos_hbm, tos, s_loc.at[1]).start()

    pl.semaphore_wait(bar, 18)
    arrived(ftv, s_loc.at[0])

    @pl.when(edge)
    def _():
        low = jnp.where(zl == 0, 4, 3)
        up = jnp.where(zl == 0, 1, -1)

        for j in range(4):
            z = low + up * j

            @pl.when(k == wk)
            def _():
                push(ftv.at[:, lax.rem(y, 2) * 8 + z], colf.at[:, zh * 4 + x], q_in.at[0], s_c4, dev(oz, x, k, y, z))

        for j in range(4):
            push(ftv.at[y, pl.ds(oz * 8, 8)], far, q_in.at[1], s_far, dev(oz, x, k, y, low + up * j))

    @pl.when(k == wk)
    def _():
        for to in plane:
            push(ftv.at[:, c16], colf.at[:, zh * 4 + x], q_in.at[2], s_col, to)

    for to, t in zip(plane, plane_tile, strict=True):
        push(ftv.at[:, t], rowf.at[:, r], q_in.at[3], s_row, to)

    for to in line + ys:
        tell(ready.at[0], to)
    rowf[:, r] = ftv[:, r]

    @pl.when(k == wk)
    def _():
        colf[:, zh * 4 + x] = ftv[:, c16]

    arrived(tos, s_loc.at[1])
    sub = lax.broadcasted_iota(I32, (16, 128), 0)
    tile = jnp.zeros((16, 128), I32)
    for a in range(16):
        tile = jnp.where(sub == a, tos[a * 16 + r], tile)

    for j in range(8):
        arrived(adj.at[pl.ds(2 * j, 2)], s_adj.at[j])

    @pl.when(r == c16)
    def _():
        tri = lax.broadcasted_iota(I32, (128, 128), 0) >= lax.broadcasted_iota(I32, (128, 128), 1)
        for b in range(8):
            a = 2 * b + c // 16
            adj[a, b] = jnp.where(tri, adj[a, b].astype(F32), 0.0).astype(BF16)

    acc[...] = jnp.zeros_like(acc)

    def col_side(h):
        for u in range(4):
            b = (zh if h == 0 else oz) * 4 + u
            w = slice(u * 128, (u + 1) * 128)
            f = colf[:, b].reshape(32, 128)
            ok = (tile > tos[b * 32 + c]) | (sub * 16 + r == b * 32 + c)
            cop[h, :, w] = col_operand(f, jnp.where(ok, 0.0, FAR)).astype(BF16)
            s1, s2 = sides(f)
            ctt[h, u * 128 : (u + 1) * 128, :] = s1.T.astype(BF16)
            ctt[h, 512 + u * 128 : 512 + (u + 1) * 128, :] = s2.T.astype(BF16)

    def row_side(i, half):
        for t in range(2):
            a = half * 8 + 2 * order(i) + t
            f = rowf[:, a].reshape(32, 128)
            lhs[i, t * 128 : (t + 1) * 128, :] = row_operand(f, a).T.astype(BF16)
            s1, s2 = sides(f)
            gb[i, :, t * 128 : (t + 1) * 128] = s1[:80].astype(BF16)
            gb[i, :, 256 + t * 128 : 256 + (t + 1) * 128] = s2[:80].astype(BF16)

    def quarter(i, half, h):
        a0 = half * 8 + 2 * order(i)
        b0 = (zh if h == 0 else oz) * 4
        e = jnp.exp2(dot(lhs[i], cop[h]))
        ad = jnp.concatenate([jnp.concatenate([adj[a0 + t, b0 + u] for u in range(4)], axis=1) for t in range(2)], axis=0)
        w = ad.astype(F32) * e
        wh = w.astype(BF16)
        wl = (w - wh.astype(F32)).astype(BF16)
        acc[h] += dot(gb[i], jnp.concatenate([wh, wl], axis=0))
        return dot(jnp.concatenate([wh, wl], axis=1), ctt[h])

    def finish_rows(i, half, p):
        a0 = half * 8 + 2 * order(i)
        for t in range(2):
            q = p[t * 128 : (t + 1) * 128].T
            f = rowf[:, a0 + t].reshape(32, 128)
            rowp[:, a0 + t] = (q[64:65] * f - q[0:32] - q[32:64]).reshape(4, 8, 128)
        two = pl.ds(a0, 2)
        for d in range(1, 4):
            push(rowp.at[lax.rem(y + d, 4), two], yrecv.at[d - 1, two], q_yr.at[a0 // 2], s_yr.at[a0 // 2], ys[d - 1])

    def settle(i, half):
        a0 = half * 8 + 2 * order(i)
        two = pl.ds(a0, 2)
        arrived(yrecv.at[:, two], s_yr.at[a0 // 2])
        ysum[two] = (rowp[y, two] + yrecv[0, two]) + (yrecv[1, two] + yrecv[2, two])
        for t in range(2):
            a = a0 + t
            here = (a == r) & (zl == base(zh) + pi)

            @pl.when(here)
            def _():
                cp = pltpu.make_async_copy(ysum.at[a], zrecv.at[rho, zl], s_loc.at[2])
                cp.start()
                cp.wait()

            @pl.when(jnp.logical_not(here))
            def _():
                push(ysum.at[a], zrecv.at[rho, zl], q_z, s_z, (a, y * 8 + base(half) + pi))

    arrived(rowf.at[:, pl.ds(zh * 8, 7)], s_row)

    @pl.when(k == wk)
    def _():
        arrived(colf.at[:, pl.ds(0, 3)], s_col)

    @pl.when(k != wk)
    def _():
        arrived(colf.at[:, pl.ds(0, 4)], s_col)

    col_side(0)

    @pl.when(k == wk)
    def _():
        arrived(colf.at[:, oz * 4 + x], s_c4)
        for to in plane:
            push(colf.at[:, oz * 4 + x], colf.at[:, oz * 4 + x], q_in.at[4], s_c5, to)

    def own_own(i, _):
        row_side(i, zh)
        prow[i] = quarter(i, zh, 0)
        return 0

    lax.fori_loop(0, 4, own_own, 0, unroll=4)

    pl.semaphore_wait(ready.at[0], 11)

    arrived(far, s_far)
    oth = oz * 8 + x * 2 + k
    rowf[y, oth] = far[x * 2 + k]
    spots = [(x * 2 + k, (r, c))] + [(t - zh * 8, to) for to, t in zip(plane, plane_tile, strict=True)]
    for spot, to in spots:
        for d in range(4):
            if spot is not spots[0][0] or d:
                push(far.at[spot], rowf.at[y, oth], q_in.at[5], s_oth, (to[0], lax.rem(y + d, 4) * 8 + zl))

    for to in plane + ys:
        tell(ready.at[1], to)

    @pl.when(k == wk)
    def _():
        arrived(colf.at[:, pl.ds(0, 3)], s_c5)

    @pl.when(k != wk)
    def _():
        arrived(colf.at[:, pl.ds(0, 4)], s_c5)

    col_side(1)

    def own_other(i, _):
        finish_rows(i, zh, prow[i] + quarter(i, zh, 1))
        return 0

    lax.fori_loop(0, 4, own_other, 0, unroll=4)

    arrived(yrecv.reshape(48, 8, 128).at[pl.ds(0, 31)], s_oth)

    def other_other(i, _):
        row_side(i, oz)
        prow[i] = quarter(i, oz, 1)
        return 0

    lax.fori_loop(0, 4, other_other, 0, unroll=4)

    def col_terms(h):
        half = zh if h == 0 else oz
        for u in range(4):
            q = acc[h, :, u * 128 : (u + 1) * 128]
            f = colf[:, half * 4 + u].reshape(32, 128)
            colp[h, :, u] = (q[64:65] * f - q[0:32] - q[32:64]).reshape(4, 8, 128)

        @pl.when(k != wk)
        def _():
            push(colp.at[h], krecv.at[h], q_k.at[h], s_k.at[h], dev(zh, x, wk, y, zl))

    def col_x(h):
        @pl.when(k == wk)
        def _():
            arrived(krecv.at[h], s_k.at[h])
            csum[h] = colp[h] + krecv[h]
            for d in range(1, 4):
                px = lax.rem(x + d, 4)
                push(csum.at[h, :, px], xrecv.at[h, d - 1], q_x.at[h], s_x.at[h], dev(zh, px, k, y, zl))

    def col_out(h):
        half = zh if h == 0 else oz

        @pl.when(k == wk)
        def _():
            arrived(xrecv.at[h], s_x.at[h])
            c2[h] = (csum[h, :, x] + xrecv[h, 0]) + (xrecv[h, 1] + xrecv[h, 2])
            for g in range(4):
                here = (y == g) & (zl == base(zh) + cpi) if h == 0 else None
                to = dev(half, x, k, g, base(half) + cpi)
                if h == 0:
                    @pl.when(here)
                    def _():
                        cp = pltpu.make_async_copy(c2.at[h, g], crecv.at[crho, zh], s_loc.at[3])
                        cp.start()
                        cp.wait()

                    @pl.when(jnp.logical_not(here))
                    def _():
                        push(c2.at[h, g], crecv.at[crho, zh], q_c, s_c, to)
                else:
                    push(c2.at[h, g], crecv.at[crho, zh], q_c, s_c, to)

    col_terms(1)
    pl.semaphore_wait(ready.at[1], 10)

    def other_own(i, _):
        finish_rows(i, oz, prow[i] + quarter(i, oz, 0))

        @pl.when(i == 1)
        def _():
            col_x(1)
        settle(i, zh)
        return 0

    lax.fori_loop(0, 4, other_own, 0, unroll=4)

    col_terms(0)
    col_x(0)

    settle(0, oz)
    settle(1, oz)

    col_out(1)

    settle(2, oz)
    settle(3, oz)

    col_out(0)

    @pl.when(final)
    def _():
        @pl.when(pi == place)
        def _():
            arrived(zrecv.reshape(NS * 8, 8, 128).at[pl.ds(0, NS * 8 - 1)], s_z)

        @pl.when(pi != place)
        def _():
            arrived(zrecv, s_z)

        @pl.when((k == wk) & (cpi == place))
        def _():
            arrived(crecv.reshape(NS * 2, 8, 128).at[pl.ds(0, NS * 2 - 1)], s_c)

        @pl.when((k != wk) | (cpi != place))
        def _():
            arrived(crecv, s_c)

        for q in range(NS):
            t = crecv[q, 0] + crecv[q, 1]
            for z in range(8):
                t = t + zrecv[q, z]
            fin[q] = -0.5 * t
            zbuf[q, place] = -0.5 * t
        for z in range(8):
            @pl.when(zl != z)
            def _():
                push(fin, zbuf.at[:, place], q_ag.at[0], s_ag.at[place], dev(zh, x, k, y, z))
        for d in range(1, 4):
            push(fin, out.at[y, :, place], q_ag.at[1], s_out.at[d - 1], ys[d - 1])

    for j in range(NP):
        @pl.when(zl != base(zh) + j)
        def _():
            arrived(zbuf.at[:, j], s_ag.at[j])
            for d in range(1, 4):
                push(zbuf.at[:, j], out.at[y, :, j], q_ag.at[1], s_out.at[d - 1], ys[d - 1])

    pltpu.make_async_copy(zbuf, out.at[y], s_loc.at[4]).start()
    for d in range(1, 4):
        arrived(out.at[lax.rem(y + 4 - d, 4)], s_out.at[d - 1])

    arrived(zbuf, s_loc.at[4])

    @pl.when(edge)
    def _():
        @pl.when(k == wk)
        def _():
            arrived(colf.at[:, pl.ds(0, 4)], q_in.at[0])
        arrived(rowf.at[:, pl.ds(0, 8)], q_in.at[1])

    @pl.when(k == wk)
    def _():
        arrived(colf.at[:, pl.ds(0, 7)], q_in.at[2])
        arrived(colf.at[:, pl.ds(0, 7)], q_in.at[4])
        for h in range(2):
            arrived(xrecv.at[h], q_x.at[h])

    @pl.when(k != wk)
    def _():
        for h in range(2):
            arrived(krecv.at[h], q_k.at[h])
    arrived(colf.at[:, pl.ds(0, 7)], q_in.at[3])
    arrived(yrecv.reshape(48, 8, 128).at[pl.ds(0, 31)], q_in.at[5])
    for j in range(8):
        arrived(yrecv.at[:, pl.ds(0, 2)], q_yr.at[j])

    @pl.when(zl == base(zh) + pi)
    def _():
        arrived(ysum.at[pl.ds(0, 15)], q_z)

    @pl.when(zl != base(zh) + pi)
    def _():
        arrived(ysum, q_z)

    @pl.when((k == wk) & (zl == base(zh) + cpi))
    def _():
        arrived(c2.reshape(8, 8, 128).at[pl.ds(0, 7)], q_c)

    @pl.when((k == wk) & (zl != base(zh) + cpi))
    def _():
        arrived(c2, q_c)

    @pl.when(final)
    def _():
        arrived(zrecv.reshape(NS * 8, 8, 128).at[pl.ds(0, NS * 7)], q_ag.at[0])
    arrived(out.at[pl.ds(0, 3)], q_ag.at[1])


def per_device(adjoint, features, tile_of_slot):
    ft = features.T.reshape(4, 8, 16, 128).transpose(0, 2, 1, 3)
    adj = adjoint.reshape(16, 8, 128, 128)
    anyspace = pl.BlockSpec(memory_space=pl.ANY)
    dma, vm = pltpu.SemaphoreType.DMA, pltpu.VMEM
    out = pl.pallas_call(
        kernel,
        out_shape=jax.ShapeDtypeStruct((4, NS, NP, 8, 128), F32),
        in_specs=[anyspace] * 3,
        out_specs=anyspace,
        scratch_shapes=[
            pltpu.SMEM((256,), I32),
            vm((16, 8, 128, 128), BF16),
            vm((4, 16, 8, 128), F32),
            vm((4, 16, 8, 128), F32),
            vm((4, 8, 8, 128), F32),
            vm((8, 8, 128), F32),
            vm((NS, NP, 8, 128), F32),
            vm((2, 256, 512), BF16),
            vm((2, 1024, 128), BF16),
            vm((4, 256, 256), BF16),
            vm((4, 80, 512), BF16),
            vm((2, 80, 512), F32),
            vm((4, 256, 128), F32),
            vm((4, 16, 8, 128), F32),
            vm((3, 16, 8, 128), F32),
            vm((16, 8, 128), F32),
            vm((NS, 8, 8, 128), F32),
            vm((2, 4, 4, 8, 128), F32),
            vm((2, 4, 4, 8, 128), F32),
            vm((2, 4, 4, 8, 128), F32),
            vm((2, 3, 4, 8, 128), F32),
            vm((2, 4, 8, 128), F32),
            vm((NS, 2, 8, 128), F32),
            vm((NS, 8, 128), F32),
            dma((8,)), dma((5,)), dma, dma, dma, dma, dma, dma, dma((8,)), dma, dma((2,)), dma((2,)), dma, dma((NP,)), dma((3,)),
            dma((6,)), dma((8,)), dma, dma((2,)), dma((2,)), dma, dma((2,)), pltpu.SemaphoreType.REGULAR((2,)),
        ],
        compiler_params=pltpu.CompilerParams(collective_id=0, has_side_effects=True, vmem_limit_bytes=60 << 20),
        cost_estimate=pl.CostEstimate(flops=5 * 2**30, bytes_accessed=5 << 20, transcendentals=2 << 20),
        name="gradient",
    )(tile_of_slot, ft, adj)
    return out.reshape(4, 16, 8, 128).transpose(0, 2, 1, 3).reshape(32, 2048).T


def solution(mesh):
    return jax.shard_map(
        per_device,
        mesh=mesh,
        in_specs=(P("row", None, "col", None, None, None), P("row", None), P()),
        out_specs=P("row", None),
        check_vma=False,
    )
```

```python
import functools
import math

import jax
import jax.numpy as jnp
from jax import lax
from jax.experimental import pallas as pl
from jax.experimental.pallas import tpu as pltpu
from jax.sharding import PartitionSpec as P

F32, BF16, I32 = jnp.float32, jnp.bfloat16, jnp.int32
MESH = pl.DeviceIdType.MESH
C0 = 0.5 * math.log2(math.e)
C1 = 0.25 * math.log2(math.e)
NP = 4
NS = 16 // NP
FAR = -1e30


def split3(x):
    h = x.astype(BF16).astype(F32)
    m = (x - h).astype(BF16).astype(F32)
    return h, m, (x - h - m).astype(BF16).astype(F32)


def pick(rows, n):
    sub = lax.broadcasted_iota(I32, (8, n), 0)
    out = jnp.zeros((8, n), F32)
    for k, v in enumerate(rows):
        out = jnp.where(sub == k, v, out)
    return out


def row_operand(f, a):
    h, m, l = split3(C0 * f)
    s = split3(-C1 * jnp.sum(f * f, axis=0, keepdims=True))
    one = jnp.ones_like(s[0])
    hot = (lax.broadcasted_iota(I32, (16, 128), 0) == a).astype(F32)
    return jnp.concatenate([h, h, m, h, m, l, pick([*s, one, one, one], 128), hot, jnp.zeros((40, 128), F32)], axis=0)


def col_operand(f, pen):
    h, m, l = split3(f)
    s = split3(-C1 * jnp.sum(f * f, axis=0, keepdims=True))
    one = jnp.ones_like(s[0])
    return jnp.concatenate([h, m, h, l, m, h, pick([one, one, one, *s], 128), pen, jnp.zeros((40, 128), F32)], axis=0)


def sides(f):
    h, m, _ = split3(f)
    one = pick([jnp.ones((1, 128), F32)], 128)
    pad = jnp.zeros((56, 128), F32)
    return jnp.concatenate([h, m, one, pad], axis=0), jnp.concatenate([h, jnp.zeros((32, 128), F32), one, pad], axis=0)


def dot(a, b):
    return lax.dot_general(a, b, (((1,), (0,)), ((), ())), preferred_element_type=F32)


def base(zh):
    return 1 + zh


def dev(zh, x, k, y, zl):
    return (zh * 8 + x * 2 + k, y * 8 + zl)


def push(src, dst, ss, rs, to):
    pltpu.make_async_remote_copy(
        src_ref=src, dst_ref=dst, send_sem=ss, recv_sem=rs, device_id=to, device_id_type=MESH
    ).start()


def arrived(ref, sem):
    pltpu.make_async_copy(ref, ref, sem).wait()


def kernel(
    tos_hbm, ft, adj_hbm, out,
    tos, adj, ftv, rowf, colf, far, zbuf, cop, ctt, lhs, gb, acc, prow, rowp, yrecv, ysum, zrecv, colp, krecv, csum, xrecv, c2, crecv, fin,
    s_adj, s_loc, s_row, s_col, s_c4, s_c5, s_far, s_oth, s_yr, s_z, s_k, s_x, s_c, s_ag, s_out,
    q_in, q_yr, q_z, q_k, q_x, q_c, q_ag, ready,
):
    r = lax.axis_index("row")
    c = lax.axis_index("col")
    zh, x, k = r // 8, lax.rem(r // 2, 4), lax.rem(r, 2)
    y, zl = c // 8, lax.rem(c, 8)
    c16 = lax.rem(c, 16)
    wk = y // 2
    oz = 1 - zh
    pi, rho = lax.rem(r, NP), r // NP
    cpi, crho = lax.rem(c16, NP), c16 // NP
    place = zl - base(zh)
    final = (place >= 0) & (place < NP)
    edge = (zl == 0) | (zl == 7)
    plane = [dev(zh, lax.rem(x + d // 2, 4), lax.rem(k + d, 2), y, zl) for d in range(1, 8)]
    plane_tile = [zh * 8 + lax.rem(x + d // 2, 4) * 2 + lax.rem(k + d, 2) for d in range(1, 8)]
    ys = [dev(zh, x, k, lax.rem(y + d, 4), zl) for d in range(1, 4)]
    def order(i):
        return lax.rem(x + jnp.where(i == 0, 2, jnp.where(i == 1, 1, jnp.where(i == 2, 3, 0))), 4)

    line = []
    for d in (4, 3, 2, 1):
        for z in (lax.rem(zh * 8 + zl + d, 16), lax.rem(zh * 8 + zl + 16 - d, 16)):
            line.append(dev(z // 8, x, k, y, lax.rem(z, 8)))

    bar = pltpu.get_barrier_semaphore()

    def tell(sem, to):
        pl.semaphore_signal(sem, inc=1, device_id=to, device_id_type=MESH)

    for to in line + ys + plane:
        tell(bar, to)
    for j in range(8):
        pltpu.make_async_copy(adj_hbm.at[pl.ds(2 * j, 2)], adj.at[pl.ds(2 * j, 2)], s_adj.at[j]).start()
    pltpu.make_async_copy(ft, ftv, s_loc.at[0]).start()
    pltpu.make_async_copy(tos_hbm, tos, s_loc.at[1]).start()

    pl.semaphore_wait(bar, 18)
    arrived(ftv, s_loc.at[0])

    @pl.when(edge)
    def _():
        low = jnp.where(zl == 0, 4, 3)
        up = jnp.where(zl == 0, 1, -1)

        for j in range(4):
            z = low + up * j

            @pl.when(k == wk)
            def _():
                push(ftv.at[:, lax.rem(y, 2) * 8 + z], colf.at[:, zh * 4 + x], q_in.at[0], s_c4, dev(oz, x, k, y, z))

        for j in range(4):
            push(ftv.at[y, pl.ds(oz * 8, 8)], far, q_in.at[1], s_far, dev(oz, x, k, y, low + up * j))

    @pl.when(k == wk)
    def _():
        for to in plane:
            push(ftv.at[:, c16], colf.at[:, zh * 4 + x], q_in.at[2], s_col, to)

    for to, t in zip(plane, plane_tile, strict=True):
        push(ftv.at[:, t], rowf.at[:, r], q_in.at[3], s_row, to)

    for to in line + ys:
        tell(ready.at[0], to)
    rowf[:, r] = ftv[:, r]

    @pl.when(k == wk)
    def _():
        colf[:, zh * 4 + x] = ftv[:, c16]

    arrived(tos, s_loc.at[1])
    sub = lax.broadcasted_iota(I32, (16, 128), 0)
    tile = jnp.zeros((16, 128), I32)
    for a in range(16):
        tile = jnp.where(sub == a, tos[a * 16 + r], tile)

    for j in range(8):
        arrived(adj.at[pl.ds(2 * j, 2)], s_adj.at[j])

    @pl.when(r == c16)
    def _():
        tri = lax.broadcasted_iota(I32, (128, 128), 0) >= lax.broadcasted_iota(I32, (128, 128), 1)
        for b in range(8):
            a = 2 * b + c // 16
            adj[a, b] = jnp.where(tri, adj[a, b].astype(F32), 0.0).astype(BF16)

    acc[...] = jnp.zeros_like(acc)

    def col_side(h):
        for u in range(4):
            b = (zh if h == 0 else oz) * 4 + u
            w = slice(u * 128, (u + 1) * 128)
            f = colf[:, b].reshape(32, 128)
            ok = (tile > tos[b * 32 + c]) | (sub * 16 + r == b * 32 + c)
            cop[h, :, w] = col_operand(f, jnp.where(ok, 0.0, FAR)).astype(BF16)
            s1, s2 = sides(f)
            ctt[h, u * 128 : (u + 1) * 128, :] = s1.T.astype(BF16)
            ctt[h, 512 + u * 128 : 512 + (u + 1) * 128, :] = s2.T.astype(BF16)

    def row_side(i, half):
        for t in range(2):
            a = half * 8 + 2 * order(i) + t
            f = rowf[:, a].reshape(32, 128)
            lhs[i, t * 128 : (t + 1) * 128, :] = row_operand(f, a).T.astype(BF16)
            s1, s2 = sides(f)
            gb[i, :, t * 128 : (t + 1) * 128] = s1[:80].astype(BF16)
            gb[i, :, 256 + t * 128 : 256 + (t + 1) * 128] = s2[:80].astype(BF16)

    def quarter(i, half, h):
        a0 = half * 8 + 2 * order(i)
        b0 = (zh if h == 0 else oz) * 4
        e = jnp.exp2(dot(lhs[i], cop[h]))
        ad = jnp.concatenate([jnp.concatenate([adj[a0 + t, b0 + u] for u in range(4)], axis=1) for t in range(2)], axis=0)
        w = ad.astype(F32) * e
        wh = w.astype(BF16)
        wl = (w - wh.astype(F32)).astype(BF16)
        acc[h] += dot(gb[i], jnp.concatenate([wh, wl], axis=0))
        return dot(jnp.concatenate([wh, wl], axis=1), ctt[h])

    def finish_rows(i, half, p):
        a0 = half * 8 + 2 * order(i)
        for t in range(2):
            q = p[t * 128 : (t + 1) * 128].T
            f = rowf[:, a0 + t].reshape(32, 128)
            rowp[:, a0 + t] = (q[64:65] * f - q[0:32] - q[32:64]).reshape(4, 8, 128)
        two = pl.ds(a0, 2)
        for d in range(1, 4):
            push(rowp.at[lax.rem(y + d, 4), two], yrecv.at[d - 1, two], q_yr.at[a0 // 2], s_yr.at[a0 // 2], ys[d - 1])

    def settle(i, half):
        a0 = half * 8 + 2 * order(i)
        two = pl.ds(a0, 2)
        arrived(yrecv.at[:, two], s_yr.at[a0 // 2])
        ysum[two] = (rowp[y, two] + yrecv[0, two]) + (yrecv[1, two] + yrecv[2, two])
        for t in range(2):
            a = a0 + t
            here = (a == r) & (zl == base(zh) + pi)

            @pl.when(here)
            def _():
                cp = pltpu.make_async_copy(ysum.at[a], zrecv.at[rho, zl], s_loc.at[2])
                cp.start()
                cp.wait()

            @pl.when(jnp.logical_not(here))
            def _():
                push(ysum.at[a], zrecv.at[rho, zl], q_z, s_z, (a, y * 8 + base(half) + pi))

    arrived(rowf.at[:, pl.ds(zh * 8, 7)], s_row)

    @pl.when(k == wk)
    def _():
        arrived(colf.at[:, pl.ds(0, 3)], s_col)

    @pl.when(k != wk)
    def _():
        arrived(colf.at[:, pl.ds(0, 4)], s_col)

    col_side(0)

    @pl.when(k == wk)
    def _():
        arrived(colf.at[:, oz * 4 + x], s_c4)
        for to in plane:
            push(colf.at[:, oz * 4 + x], colf.at[:, oz * 4 + x], q_in.at[4], s_c5, to)

    def own_own(i, _):
        row_side(i, zh)
        prow[i] = quarter(i, zh, 0)
        return 0

    lax.fori_loop(0, 2, own_own, 0, unroll=2)

    pl.semaphore_wait(ready.at[0], 11)

    arrived(far, s_far)
    oth = oz * 8 + x * 2 + k
    rowf[y, oth] = far[x * 2 + k]
    spots = [(x * 2 + k, (r, c))] + [(t - zh * 8, to) for to, t in zip(plane, plane_tile, strict=True)]
    for spot, to in spots:
        for d in range(4):
            if spot is not spots[0][0] or d:
                push(far.at[spot], rowf.at[y, oth], q_in.at[5], s_oth, (to[0], lax.rem(y + d, 4) * 8 + zl))

    lax.fori_loop(2, 4, own_own, 0, unroll=2)

    for to in plane + ys:
        tell(ready.at[1], to)

    @pl.when(k == wk)
    def _():
        arrived(colf.at[:, pl.ds(0, 3)], s_c5)

    @pl.when(k != wk)
    def _():
        arrived(colf.at[:, pl.ds(0, 4)], s_c5)

    col_side(1)

    def own_other(i, _):
        finish_rows(i, zh, prow[i] + quarter(i, zh, 1))
        return 0

    lax.fori_loop(0, 4, own_other, 0, unroll=4)

    arrived(yrecv.reshape(48, 8, 128).at[pl.ds(0, 31)], s_oth)

    def other_other(i, _):
        row_side(i, oz)
        prow[i] = quarter(i, oz, 1)
        return 0

    lax.fori_loop(0, 4, other_other, 0, unroll=4)

    def col_terms(h):
        half = zh if h == 0 else oz
        for u in range(4):
            q = acc[h, :, u * 128 : (u + 1) * 128]
            f = colf[:, half * 4 + u].reshape(32, 128)
            colp[h, :, u] = (q[64:65] * f - q[0:32] - q[32:64]).reshape(4, 8, 128)

        @pl.when(k != wk)
        def _():
            push(colp.at[h], krecv.at[h], q_k.at[h], s_k.at[h], dev(zh, x, wk, y, zl))

    def col_x(h):
        @pl.when(k == wk)
        def _():
            arrived(krecv.at[h], s_k.at[h])
            csum[h] = colp[h] + krecv[h]
            for d in range(1, 4):
                px = lax.rem(x + d, 4)
                push(csum.at[h, :, px], xrecv.at[h, d - 1], q_x.at[h], s_x.at[h], dev(zh, px, k, y, zl))

    def col_out(h):
        half = zh if h == 0 else oz

        @pl.when(k == wk)
        def _():
            arrived(xrecv.at[h], s_x.at[h])
            c2[h] = (csum[h, :, x] + xrecv[h, 0]) + (xrecv[h, 1] + xrecv[h, 2])
            for g in range(4):
                here = (y == g) & (zl == base(zh) + cpi) if h == 0 else None
                to = dev(half, x, k, g, base(half) + cpi)
                if h == 0:
                    @pl.when(here)
                    def _():
                        cp = pltpu.make_async_copy(c2.at[h, g], crecv.at[crho, zh], s_loc.at[3])
                        cp.start()
                        cp.wait()

                    @pl.when(jnp.logical_not(here))
                    def _():
                        push(c2.at[h, g], crecv.at[crho, zh], q_c, s_c, to)
                else:
                    push(c2.at[h, g], crecv.at[crho, zh], q_c, s_c, to)

    col_terms(1)
    pl.semaphore_wait(ready.at[1], 10)

    def other_own(i, _):
        finish_rows(i, oz, prow[i] + quarter(i, oz, 0))

        @pl.when(i == 1)
        def _():
            col_x(1)
        settle(i, zh)
        return 0

    lax.fori_loop(0, 4, other_own, 0, unroll=4)

    col_terms(0)
    col_x(0)

    settle(0, oz)
    settle(1, oz)

    col_out(1)

    settle(2, oz)
    settle(3, oz)

    col_out(0)

    @pl.when(final)
    def _():
        @pl.when(pi == place)
        def _():
            arrived(zrecv.reshape(NS * 8, 8, 128).at[pl.ds(0, NS * 8 - 1)], s_z)

        @pl.when(pi != place)
        def _():
            arrived(zrecv, s_z)

        @pl.when((k == wk) & (cpi == place))
        def _():
            arrived(crecv.reshape(NS * 2, 8, 128).at[pl.ds(0, NS * 2 - 1)], s_c)

        @pl.when((k != wk) | (cpi != place))
        def _():
            arrived(crecv, s_c)

        for q in range(NS):
            t = crecv[q, 0] + crecv[q, 1]
            for z in range(8):
                t = t + zrecv[q, z]
            fin[q] = -0.5 * t
            zbuf[q, place] = -0.5 * t
        for z in range(8):
            @pl.when(zl != z)
            def _():
                push(fin, zbuf.at[:, place], q_ag.at[0], s_ag.at[place], dev(zh, x, k, y, z))
        for d in range(1, 4):
            push(fin, out.at[y, :, place], q_ag.at[1], s_out.at[d - 1], ys[d - 1])

    for j in range(NP):
        @pl.when(zl != base(zh) + j)
        def _():
            arrived(zbuf.at[:, j], s_ag.at[j])
            for d in range(1, 4):
                push(zbuf.at[:, j], out.at[y, :, j], q_ag.at[1], s_out.at[d - 1], ys[d - 1])

    pltpu.make_async_copy(zbuf, out.at[y], s_loc.at[4]).start()
    for d in range(1, 4):
        arrived(out.at[lax.rem(y + 4 - d, 4)], s_out.at[d - 1])

    arrived(zbuf, s_loc.at[4])

    @pl.when(edge)
    def _():
        @pl.when(k == wk)
        def _():
            arrived(colf.at[:, pl.ds(0, 4)], q_in.at[0])
        arrived(rowf.at[:, pl.ds(0, 8)], q_in.at[1])

    @pl.when(k == wk)
    def _():
        arrived(colf.at[:, pl.ds(0, 7)], q_in.at[2])
        arrived(colf.at[:, pl.ds(0, 7)], q_in.at[4])
        for h in range(2):
            arrived(xrecv.at[h], q_x.at[h])

    @pl.when(k != wk)
    def _():
        for h in range(2):
            arrived(krecv.at[h], q_k.at[h])
    arrived(colf.at[:, pl.ds(0, 7)], q_in.at[3])
    arrived(yrecv.reshape(48, 8, 128).at[pl.ds(0, 31)], q_in.at[5])
    for j in range(8):
        arrived(yrecv.at[:, pl.ds(0, 2)], q_yr.at[j])

    @pl.when(zl == base(zh) + pi)
    def _():
        arrived(ysum.at[pl.ds(0, 15)], q_z)

    @pl.when(zl != base(zh) + pi)
    def _():
        arrived(ysum, q_z)

    @pl.when((k == wk) & (zl == base(zh) + cpi))
    def _():
        arrived(c2.reshape(8, 8, 128).at[pl.ds(0, 7)], q_c)

    @pl.when((k == wk) & (zl != base(zh) + cpi))
    def _():
        arrived(c2, q_c)

    @pl.when(final)
    def _():
        arrived(zrecv.reshape(NS * 8, 8, 128).at[pl.ds(0, NS * 7)], q_ag.at[0])
    arrived(out.at[pl.ds(0, 3)], q_ag.at[1])


def per_device(adjoint, features, tile_of_slot):
    ft = features.T.reshape(4, 8, 16, 128).transpose(0, 2, 1, 3)
    adj = adjoint.reshape(16, 8, 128, 128)
    anyspace = pl.BlockSpec(memory_space=pl.ANY)
    dma, vm = pltpu.SemaphoreType.DMA, pltpu.VMEM
    out = pl.pallas_call(
        kernel,
        out_shape=jax.ShapeDtypeStruct((4, NS, NP, 8, 128), F32),
        in_specs=[anyspace] * 3,
        out_specs=anyspace,
        scratch_shapes=[
            pltpu.SMEM((256,), I32),
            vm((16, 8, 128, 128), BF16),
            vm((4, 16, 8, 128), F32),
            vm((4, 16, 8, 128), F32),
            vm((4, 8, 8, 128), F32),
            vm((8, 8, 128), F32),
            vm((NS, NP, 8, 128), F32),
            vm((2, 256, 512), BF16),
            vm((2, 1024, 128), BF16),
            vm((4, 256, 256), BF16),
            vm((4, 80, 512), BF16),
            vm((2, 80, 512), F32),
            vm((4, 256, 128), F32),
            vm((4, 16, 8, 128), F32),
            vm((3, 16, 8, 128), F32),
            vm((16, 8, 128), F32),
            vm((NS, 8, 8, 128), F32),
            vm((2, 4, 4, 8, 128), F32),
            vm((2, 4, 4, 8, 128), F32),
            vm((2, 4, 4, 8, 128), F32),
            vm((2, 3, 4, 8, 128), F32),
            vm((2, 4, 8, 128), F32),
            vm((NS, 2, 8, 128), F32),
            vm((NS, 8, 128), F32),
            dma((8,)), dma((5,)), dma, dma, dma, dma, dma, dma, dma((8,)), dma, dma((2,)), dma((2,)), dma, dma((NP,)), dma((3,)),
            dma((6,)), dma((8,)), dma, dma((2,)), dma((2,)), dma, dma((2,)), pltpu.SemaphoreType.REGULAR((2,)),
        ],
        compiler_params=pltpu.CompilerParams(collective_id=0, has_side_effects=True, vmem_limit_bytes=60 << 20),
        cost_estimate=pl.CostEstimate(flops=5 * 2**30, bytes_accessed=5 << 20, transcendentals=2 << 20),
        name="gradient",
    )(tile_of_slot, ft, adj)
    return out.reshape(4, 16, 8, 128).transpose(0, 2, 1, 3).reshape(32, 2048).T


def solution(mesh):
    return jax.shard_map(
        per_device,
        mesh=mesh,
        in_specs=(P("row", None, "col", None, None, None), P("row", None), P()),
        out_specs=P("row", None),
        check_vma=False,
    )
```
